32 devices in a mesh: blk: 16 (over z, y, x), mp: 2 (over core).
Axes of the slice: x: 2, y: 2, z: 4, core: 2. Of those that a mesh axis runs over, the one named last changes fastest.
Arguments:
- decoder_in: bfloat16 [8192, 768], P(('blk', 'mp')), may hold values from -6 to 6
- encoder_out: bfloat16 [2048, 768], P('blk'), may hold values from -6 to 6
- out_grad: bfloat16 [8192, 768], P(('blk', 'mp')), may hold values from -6 to 6
- block_items: int32 [32], P('blk'), may hold values from 0 to 15, as said below
- block_lengths: int32 [32], P('blk'), may hold values from 16 to 64
- target_lengths: int32 [16], P('blk'), may hold values from 128 to 512
- self_proj: float32 [3, 768, 768], P(None, 'blk', 'mp'), may hold values from -0.078125 to 0.078125
- self_out: float32 [768, 768], P('mp', 'blk'), may hold values from -1.25 to 1.25
- cross_proj: float32 [3, 768, 768], P(None, 'blk', 'mp'), may hold values from -0.078125 to 0.078125
- cross_out: float32 [768, 768], P('mp', 'blk'), may hold values from -3 to 3
- feed_in: float32 [2, 768, 2048], P(None, 'blk', 'mp'), may hold values from -0.21875 to 0.21875
- feed_out: float32 [2048, 768], P('mp', 'blk'), may hold values from -0.125 to 0.125
- norm_gains: float32 [3, 768], replicated, may hold values from 0.5 to 1.5
- position_bias: float32 [32, 12], replicated, may hold values from -3 to 3
- first_self_proj: float32 [3, 768, 768], P(None, 'blk', 'mp'), may hold values from -0.00021362305 to 0.00021362305
- first_self_out: float32 [768, 768], P('mp', 'blk'), may hold values from -2.2888184e-05 to 2.2888184e-05
- first_cross_proj: float32 [3, 768, 768], P(None, 'blk', 'mp'), may hold values from -0.00021362305 to 0.00021362305
- first_cross_out: float32 [768, 768], P('mp', 'blk'), may hold values from -1.1444092e-05 to 1.1444092e-05
- first_feed_in: float32 [2, 768, 2048], P(None, 'blk', 'mp'), may hold values from -4.5776367e-05 to 4.5776367e-05
- first_feed_out: float32 [2048, 768], P('mp', 'blk'), may hold values from -6.1035156e-05 to 6.1035156e-05
- first_gains: float32 [3, 768], replicated, may hold values from -0.00015258789 to 0.00015258789
- first_bias: float32 [32, 12], replicated, may hold values from -0.00010681152 to 0.00010681152
- second_self_proj: float32 [3, 768, 768], P(None, 'blk', 'mp'), may hold values from 1.0593364e-10 to 4.2373455e-10
- second_self_out: float32 [768, 768], P('mp', 'blk'), may hold values from 1.2712036e-12 to 5.0848145e-12
- second_cross_proj: float32 [3, 768, 768], P(None, 'blk', 'mp'), may hold values from 1.0593364e-10 to 4.2373455e-10
- second_cross_out: float32 [768, 768], P('mp', 'blk'), may hold values from 3.178009e-13 to 1.2712036e-12
- second_feed_in: float32 [2, 768, 2048], P(None, 'blk', 'mp'), may hold values from 4.2373457e-12 to 1.6949383e-11
- second_feed_out: float32 [2048, 768], P('mp', 'blk'), may hold values from 1.0593364e-11 to 4.2373455e-11
- second_gains: float32 [3, 768], replicated, may hold values from 5.296682e-11 to 2.1186727e-10
- second_bias: float32 [32, 12], replicated, may hold values from 2.4364738e-11 to 9.745895e-11
Outputs:
- layer_out: bfloat16 [8192, 768], P(('blk', 'mp'))
- decoder_grad: float32 [8192, 768], P(('blk', 'mp'))
- encoder_grad: float32 [2048, 768], P('blk', 'mp')
- new_self_proj: float32 [3, 768, 768], P(None, 'blk', 'mp')
- new_self_out: float32 [768, 768], P('mp', 'blk')
- new_cross_proj: float32 [3, 768, 768], P(None, 'blk', 'mp')
- new_cross_out: float32 [768, 768], P('mp', 'blk')
- new_feed_in: float32 [2, 768, 2048], P(None, 'blk', 'mp')
- new_feed_out: float32 [2048, 768], P('mp', 'blk')
- new_gains: float32 [3, 768], replicated
- new_bias: float32 [32, 12], replicated
- moment_self_proj: float32 [3, 768, 768], P(None, 'blk', 'mp')
- moment_self_out: float32 [768, 768], P('mp', 'blk')
- moment_cross_proj: float32 [3, 768, 768], P(None, 'blk', 'mp')
- moment_cross_out: float32 [768, 768], P('mp', 'blk')
- moment_feed_in: float32 [2, 768, 2048], P(None, 'blk', 'mp')
- moment_feed_out: float32 [2048, 768], P('mp', 'blk')
- moment_gains: float32 [3, 768], replicated
- moment_bias: float32 [32, 12], replicated
- square_self_proj: float32 [3, 768, 768], P(None, 'blk', 'mp')
- square_self_out: float32 [768, 768], P('mp', 'blk')
- square_cross_proj: float32 [3, 768, 768], P(None, 'blk', 'mp')
- square_cross_out: float32 [768, 768], P('mp', 'blk')
- square_feed_in: float32 [2, 768, 2048], P(None, 'blk', 'mp')
- square_feed_out: float32 [2048, 768], P('mp', 'blk')
- square_gains: float32 [3, 768], replicated
- square_bias: float32 [32, 12], replicated
- grad_norm: float32 [], replicated
- token_rms: float32 [2], replicated
The draws below stay inside these ranges and needn't reach their ends.
Inputs may be any that keep to these rules, and one draw needn't show every extreme that they name: `block_items`: every one of the 16 items owns at least one block.
All inputs are finite; a program needn't handle non-finite values.
Results may differ from the reference program's by a relative error of at most 0.019.
Values may be sent and summed in bfloat16 or wider, within the bound.
A program may use at most 256 MiB of HBM per device.

```python
import math
import jax
import jax.numpy as jnp
import numpy as np
from jax import lax

D = 768
H = 12
DH = 64
FF = 2048
NB = 32
DEC_LEN = 512
KB = 64
STEP = 10
ITEMS = 16
DEC_TOT = 8192
ENC_TOT = 2048
NBLOCKS = 32
NPARAMS = 9439872


def draw_block_items(key, part):
    key = jax.random.fold_in(key, 11)
    key_order, key_picks, key_place = jax.random.split(key, 3)
    order = jax.random.permutation(key_order, ITEMS).astype(jnp.int32)
    longest = order[:4]
    picks = jax.random.randint(key_picks, (NBLOCKS - 2 - ITEMS,), 0, 4)
    middle = jnp.concatenate([jnp.arange(ITEMS, dtype=jnp.int32), longest[picks]])
    middle = jax.random.permutation(key_place, middle)
    spanning = order[0:1]
    return jnp.concatenate([spanning, middle, spanning]).astype(jnp.int32)


def draw_block_lengths(key, part):
    key = jax.random.fold_in(key, 12)
    fills = jax.random.randint(key, (NBLOCKS,), KB // 4, KB + 1)
    fills = fills.at[0].set(KB)
    fills = fills.at[1].set(KB // 4)
    return fills.astype(jnp.int32)


def draw_target_lengths(key, part):
    key = jax.random.fold_in(key, 13)
    sequence = jnp.arange(ITEMS, dtype=jnp.int32)
    base = DEC_LEN // 4 + (DEC_LEN - DEC_LEN // 4) * sequence // (ITEMS - 1)
    jitter = jax.random.randint(key, (ITEMS,), 0, DEC_LEN // 8 + 1)
    jitter = jnp.where((sequence == 0) | (sequence == ITEMS - 1), 0, jitter)
    return jnp.minimum(base + jitter, DEC_LEN).astype(jnp.int32)


def shard_levels(own_key, dims, shards, smallest, high):
    level, own = 1.0, jax.random.fold_in(own_key, 6)
    for axis_at, shards_of in shards:
        draws = jnp.exp(jax.random.uniform(jax.random.fold_in(own, axis_at), (shards_of,), jnp.float32, smallest / len(shards), high / len(shards)))
        level = level * jnp.repeat(draws, dims[axis_at] // shards_of).reshape([-1 if axis == axis_at else 1 for axis in range(len(dims))])
    return level


def gaussian(stream_key, shape, scale, reach, cuts=(), kind=jnp.bfloat16):
    values = jax.random.normal(stream_key, shape, jnp.float32) * scale
    if len(cuts) > 0:
        values = shard_levels(stream_key, shape, cuts, -0.22, 0.18) * values
    return jnp.clip(values, min=-reach, max=reach).astype(kind)


def setup_inputs(seed: int = 0) -> dict:
    key_of = jax.random.split(jax.random.key(seed), 31)
    decoder_in = gaussian(key_of[0], (DEC_TOT, D), 1.0, 6.0, ((0, 32),))
    encoder_out = gaussian(key_of[1], (ENC_TOT, D), 1.0, 6.0, ((0, 16),))
    out_grad = gaussian(key_of[2], (DEC_TOT, D), 1.0, 6.0, ((0, 32),))
    block_items = draw_block_items(jax.random.fold_in(key_of[30], 71), 0)
    block_lengths = draw_block_lengths(jax.random.fold_in(key_of[30], 71), 0)
    target_lengths = draw_target_lengths(jax.random.fold_in(key_of[30], 71), 0)
    self_proj = gaussian(key_of[6], (3, D, D), (8 * D) ** -0.5, 0.078125, ((1, 16), (2, 2)), jnp.float32)
    self_out = gaussian(key_of[7], (D, D), 0.2, 1.25, ((0, 2), (1, 16)), jnp.float32)
    cross_proj = gaussian(key_of[8], (3, D, D), (8 * D) ** -0.5, 0.078125, ((1, 16), (2, 2)), jnp.float32)
    cross_out = gaussian(key_of[9], (D, D), 0.5, 3.0, ((0, 2), (1, 16)), jnp.float32)
    feed_in = gaussian(key_of[10], (2, D, FF), D ** -0.5, 0.21875, ((1, 16), (2, 2)), jnp.float32)
    feed_out = gaussian(key_of[11], (FF, D), FF ** -0.5, 0.125, ((0, 2), (1, 16)), jnp.float32)
    norm_gains = jnp.clip(1.0 + 0.1 * jax.random.normal(key_of[12], (3, D), jnp.float32), 0.5, 1.5)
    position_bias = gaussian(key_of[13], (NB, H), 0.5, 3.0, (), jnp.float32)
    first_self_proj = gaussian(key_of[14], (3, D, D), (0.11 * NPARAMS ** -0.5), 0.00021362305, ((1, 16), (2, 2)), jnp.float32)
    first_self_out = gaussian(key_of[15], (D, D), (0.012 * NPARAMS ** -0.5), 2.288818359375e-05, ((0, 2), (1, 16)), jnp.float32)
    first_cross_proj = gaussian(key_of[16], (3, D, D), (0.11 * NPARAMS ** -0.5), 0.00021362305, ((1, 16), (2, 2)), jnp.float32)
    first_cross_out = gaussian(key_of[17], (D, D), (0.006 * NPARAMS ** -0.5), 1.1444091796875e-05, ((0, 2), (1, 16)), jnp.float32)
    first_feed_in = gaussian(key_of[18], (2, D, FF), (0.022 * NPARAMS ** -0.5), 4.57763671875e-05, ((1, 16), (2, 2)), jnp.float32)
    first_feed_out = gaussian(key_of[19], (FF, D), (0.035 * NPARAMS ** -0.5), 6.103515625e-05, ((0, 2), (1, 16)), jnp.float32)
    first_gains = gaussian(key_of[20], (3, D), (0.078 * NPARAMS ** -0.5), 0.00015258789, (), jnp.float32)
    first_bias = gaussian(key_of[21], (NB, H), (0.053 * NPARAMS ** -0.5), 0.00010681152, (), jnp.float32)
    second_self_proj = jnp.clip(jnp.exp(math.log(4.237345474500387e-10) - 1.3862944 * jax.random.uniform(key_of[22], (3, D, D), jnp.float32) ** shard_levels(key_of[22], (3, D, D), ((1, 16), (2, 2)), -0.2, 0.2)), 1.0593363686250967e-10, 4.237345474500387e-10)
    second_self_out = jnp.clip(jnp.exp(math.log(5.084814513889313e-12) - 1.3862944 * jax.random.uniform(key_of[23], (D, D), jnp.float32) ** shard_levels(key_of[23], (D, D), ((0, 2), (1, 16)), -0.2, 0.2)), 1.2712036284723283e-12, 5.084814513889313e-12)
    second_cross_proj = jnp.clip(jnp.exp(math.log(4.237345474500387e-10) - 1.3862944 * jax.random.uniform(key_of[24], (3, D, D), jnp.float32) ** shard_levels(key_of[24], (3, D, D), ((1, 16), (2, 2)), -0.2, 0.2)), 1.0593363686250967e-10, 4.237345474500387e-10)
    second_cross_out = jnp.clip(jnp.exp(math.log(1.2712036284723283e-12) - 1.3862944 * jax.random.uniform(key_of[25], (D, D), jnp.float32) ** shard_levels(key_of[25], (D, D), ((0, 2), (1, 16)), -0.2, 0.2)), 3.1780090711808207e-13, 1.2712036284723283e-12)
    second_feed_in = jnp.clip(jnp.exp(math.log(1.6949382869446694e-11) - 1.3862944 * jax.random.uniform(key_of[26], (2, D, FF), jnp.float32) ** shard_levels(key_of[26], (2, D, FF), ((1, 16), (2, 2)), -0.2, 0.2)), 4.2373457173616735e-12, 1.6949382869446694e-11)
    second_feed_out = jnp.clip(jnp.exp(math.log(4.237345543889326e-11) - 1.3862944 * jax.random.uniform(key_of[27], (FF, D), jnp.float32) ** shard_levels(key_of[27], (FF, D), ((0, 2), (1, 16)), -0.2, 0.2)), 1.0593363859723315e-11, 4.237345543889326e-11)
    second_gains = jnp.clip(jnp.exp(jax.random.uniform(key_of[28], (3, D), jnp.float32, math.log(5.2966818431254836e-11), math.log(2.1186727372501934e-10))), 5.2966818431254836e-11, 2.1186727372501934e-10)
    second_bias = jnp.clip(jnp.exp(jax.random.uniform(key_of[29], (NB, H), jnp.float32, math.log(2.4364737657989188e-11), math.log(9.745895063195675e-11))), 2.4364737657989188e-11, 9.745895063195675e-11)
    return {"decoder_in": decoder_in, "encoder_out": encoder_out, "out_grad": out_grad, "block_items": block_items, "block_lengths": block_lengths, "target_lengths": target_lengths, "self_proj": self_proj, "self_out": self_out, "cross_proj": cross_proj, "cross_out": cross_out, "feed_in": feed_in, "feed_out": feed_out, "norm_gains": norm_gains, "position_bias": position_bias, "first_self_proj": first_self_proj, "first_self_out": first_self_out, "first_cross_proj": first_cross_proj, "first_cross_out": first_cross_out, "first_feed_in": first_feed_in, "first_feed_out": first_feed_out, "first_gains": first_gains, "first_bias": first_bias, "second_self_proj": second_self_proj, "second_self_out": second_self_out, "second_cross_proj": second_cross_proj, "second_cross_out": second_cross_out, "second_feed_in": second_feed_in, "second_feed_out": second_feed_out, "second_gains": second_gains, "second_bias": second_bias}


norm_eps = 1e-06
clip_limit = 1.0
learn_rates = (0.02, 0.2, 0.02, 0.5, 0.02, 0.02, 1.0, 0.5)
beta_one = 0.9
beta_two = 0.999
adam_eps = 1e-08
weight_decay = 0.01
masked_score = -1000000000.0
HIGHEST = lax.Precision.HIGHEST
edge_table = np.ceil(16.0 * 8.0 ** (np.arange(16) / 16.0)).astype(np.int32)

@jax.custom_vjp
def low(v):
    return lax.optimization_barrier(v.astype(jnp.bfloat16)).astype(jnp.float32)

@jax.custom_vjp
def low_back(v):
    return v

def low_keep(v):
    return (low(v), None)

def low_pass(kept, grad):
    return (grad,)

def back_keep(v):
    return (v, None)

def back_low(kept, grad):
    return (low(grad),)
low.defvjp(low_keep, low_pass)
low_back.defvjp(back_keep, back_low)

def matmul(left, right):
    return jnp.dot(left, right, precision=HIGHEST, preferred_element_type=jnp.float32)

def rms_norm(values, gain):
    return values * lax.rsqrt(lax.optimization_barrier(jnp.mean(values * values, axis=-1, keepdims=True)) + norm_eps) * gain

def bucket_table(length):
    places = jnp.arange(length, dtype=jnp.int32)
    distance = jnp.maximum(places[:, None] - places[None, :], 0)
    edges = jnp.asarray(edge_table)
    above = lax.optimization_barrier(jnp.sum((distance[:, :, None] >= edges[None, None, :]).astype(jnp.int32), axis=2))
    return jnp.where(distance < 16, distance, 15 + above)

def softmax_rows(scores):
    shifted = jnp.exp(scores - lax.optimization_barrier(jnp.max(scores, axis=-1, keepdims=True)))
    return shifted / lax.optimization_barrier(jnp.sum(shifted, axis=-1, keepdims=True))

def adamw(weight, moment, second, grad, decay, rate):
    moment = beta_one * moment + (1.0 - beta_one) * grad
    second = beta_two * second + (1.0 - beta_two) * grad * grad
    fixed_first = moment / (1.0 - beta_one ** STEP)
    fixed_second = second / (1.0 - beta_two ** STEP)
    weight = weight - rate * (fixed_first / (jnp.sqrt(fixed_second) + adam_eps) + decay * weight)
    return (weight, moment, second)

def layer_forward(params, tokens, encoded, tags):
    self_proj, self_out, cross_proj, cross_out, feed_in, feed_out, norm_gains, position_bias = params
    self_proj = low(self_proj)
    self_out = low(self_out)
    cross_proj = low(cross_proj)
    cross_out = low(cross_out)
    feed_in = low(feed_in)
    feed_out = low(feed_out)
    enc_keys = low(low_back(matmul(encoded, cross_proj[1]))).reshape(ENC_TOT, H, DH)
    enc_values = low(low_back(matmul(encoded, cross_proj[2]))).reshape(ENC_TOT, H, DH)
    places = jnp.arange(DEC_LEN, dtype=jnp.int32)
    causal = places[:, None] >= places[None, :]
    bias_full = jnp.transpose(position_bias[bucket_table(DEC_LEN)], (2, 0, 1))

    def one_sequence(inputs):
        rows, item = inputs
        normed = low(rms_norm(rows, norm_gains[0]))
        queries = low(low_back(matmul(normed, self_proj[0]))).reshape(DEC_LEN, H, DH)
        keys = low(low_back(matmul(normed, self_proj[1]))).reshape(DEC_LEN, H, DH)
        values = low(low_back(matmul(normed, self_proj[2]))).reshape(DEC_LEN, H, DH)
        scores = jnp.einsum('qhd,khd->hqk', queries, keys, precision=HIGHEST) + bias_full
        scores = low_back(jnp.where(causal[None], scores, masked_score))
        probs = low(softmax_rows(scores))
        attended = jnp.einsum('hqk,khd->qhd', probs, values, precision=HIGHEST).reshape(DEC_LEN, D)
        attended = low(low_back(attended))
        after_one = rows + low_back(matmul(attended, self_out))
        normed = low(rms_norm(after_one, norm_gains[1]))
        cross_queries = low(low_back(matmul(normed, cross_proj[0]))).reshape(DEC_LEN, H, DH)
        scores = jnp.einsum('qhd,khd->hqk', cross_queries, enc_keys, precision=HIGHEST)
        scores = low_back(jnp.where((tags == item)[None, None, :], scores, masked_score))
        probs = softmax_rows(scores)
        attended = jnp.einsum('hqk,khd->qhd', probs, enc_values, precision=HIGHEST).reshape(DEC_LEN, D)
        attended = low(low_back(attended))
        after_two = after_one + low_back(matmul(attended, cross_out))
        normed = low(rms_norm(after_two, norm_gains[2]))
        gate = low_back(matmul(normed, feed_in[0]))
        upper = low_back(matmul(normed, feed_in[1]))
        hidden = low(jax.nn.gelu(gate, approximate=True) * upper)
        return after_two + low_back(matmul(hidden, feed_out))
    outputs = lax.map(jax.checkpoint(one_sequence), (tokens.reshape(ITEMS, DEC_LEN, D), jnp.arange(ITEMS, dtype=jnp.int32)))
    return outputs.reshape(DEC_TOT, D)

def reference(decoder_in, encoder_out, out_grad, block_items, block_lengths, target_lengths, self_proj, self_out, cross_proj, cross_out, feed_in, feed_out, norm_gains, position_bias, first_self_proj, first_self_out, first_cross_proj, first_cross_out, first_feed_in, first_feed_out, first_gains, first_bias, second_self_proj, second_self_out, second_cross_proj, second_cross_out, second_feed_in, second_feed_out, second_gains, second_bias):
    places = jnp.arange(ENC_TOT, dtype=jnp.int32)
    tags = jnp.where(places % KB < jnp.repeat(block_lengths, KB), jnp.repeat(block_items, KB), -1)
    params = (self_proj, self_out, cross_proj, cross_out, feed_in, feed_out, norm_gains, position_bias)
    firsts = (first_self_proj, first_self_out, first_cross_proj, first_cross_out, first_feed_in, first_feed_out, first_gains, first_bias)
    seconds = (second_self_proj, second_self_out, second_cross_proj, second_cross_out, second_feed_in, second_feed_out, second_gains, second_bias)

    def forward(weights, tokens, encoded):
        return layer_forward(weights, tokens, encoded, tags)
    result, pull = jax.vjp(forward, params, decoder_in.astype(jnp.float32), encoder_out.astype(jnp.float32))
    token_place = jnp.arange(DEC_TOT, dtype=jnp.int32) % DEC_LEN
    valid = (token_place < jnp.repeat(target_lengths, DEC_LEN)).astype(jnp.float32)[:, None]
    grads, input_grad, encoder_grad = pull(out_grad.astype(jnp.float32) * valid)
    squares = sum((jnp.sum(member * member) for member in grads))
    grad_norm = jnp.sqrt(squares)
    factor = jnp.minimum(1.0, clip_limit / (grad_norm + 1e-06))
    new_weights = []
    new_firsts = []
    new_seconds = []
    for index in range(8):
        decay = weight_decay if index < 6 else 0.0
        weight, moment, second = adamw(params[index], firsts[index], seconds[index], grads[index] * factor, decay, learn_rates[index])
        new_weights.append(weight)
        new_firsts.append(moment)
        new_seconds.append(second)
    counted = jnp.sum(valid)
    token_rms = jnp.stack([jnp.sqrt(jnp.sum(valid * result * result) / (counted * D)), jnp.sqrt(jnp.sum(valid * input_grad * input_grad) / (counted * D))])
    return (result.astype(jnp.bfloat16), input_grad, encoder_grad, new_weights[0], new_weights[1], new_weights[2], new_weights[3], new_weights[4], new_weights[5], new_weights[6], new_weights[7], new_firsts[0], new_firsts[1], new_firsts[2], new_firsts[3], new_firsts[4], new_firsts[5], new_firsts[6], new_firsts[7], new_seconds[0], new_seconds[1], new_seconds[2], new_seconds[3], new_seconds[4], new_seconds[5], new_seconds[6], new_seconds[7], grad_norm, token_rms)
```

```python
import functools
import math

import jax
import jax.numpy as jnp
import numpy as np
from jax import lax
from jax.experimental import pallas as pl
from jax.experimental.pallas import tpu as pltpu
from jax.sharding import PartitionSpec as P

D = 768
DH = 64
KB = 64
STEP = 10
MESH = pl.DeviceIdType.MESH
ANY = pl.BlockSpec(memory_space=pl.ANY)
VMEM = pl.BlockSpec(memory_space=pltpu.VMEM)

norm_eps = 1e-06
clip_limit = 1.0
learn_rates = (0.02, 0.2, 0.02, 0.5, 0.02, 0.02, 1.0, 0.5)
beta_one = 0.9
beta_two = 0.999
adam_eps = 1e-08
weight_decay = 0.01
masked_score = -1000000000.0
HIGHEST = lax.Precision.HIGHEST
BF = jnp.bfloat16
F32 = jnp.float32
edge_table = np.ceil(16.0 * 8.0 ** (np.arange(16) / 16.0)).astype(np.int32)


def bucket_of(distance):
    above = np.sum(distance[..., None] >= edge_table, axis=-1)
    return np.where(distance < 16, distance, 15 + above)


def rms_norm(values, gain):
    return values * lax.rsqrt(jnp.mean(values * values, axis=-1, keepdims=True) + norm_eps) * gain


def norm_back(values, gain, upstream):
    scale = lax.rsqrt(jnp.mean(values * values, axis=-1, keepdims=True) + norm_eps)
    weighted = upstream * gain
    inner = jnp.mean(weighted * values, axis=-1, keepdims=True)
    return (
        scale * weighted - values * scale * scale * scale * inner,
        jnp.sum(upstream * values * scale, axis=0),
    )


def adamw(weight, moment, second, grad, decay, rate):
    moment = beta_one * moment + (1.0 - beta_one) * grad
    second = beta_two * second + (1.0 - beta_two) * grad * grad
    fixed_first = moment / (1.0 - beta_one**STEP)
    fixed_second = second / (1.0 - beta_two**STEP)
    weight = weight - rate * (fixed_first / (jnp.sqrt(fixed_second) + adam_eps) + decay * weight)
    return (weight, moment, second)


def toeplitz_kernel(strip_ref, out_ref):
    @pl.loop(0, strip_ref.shape[0])
    def _(index):
        rows = jnp.broadcast_to(strip_ref[index], (128, 256))
        out_ref[index] = pltpu.roll(rows, 0, 1, stride=1, stride_axis=0)[:, :128]


class Place:
    def __init__(self, levels):
        self.levels = levels
        self.long = 2**levels
        self.me = lax.axis_index("blk")
        self.core = lax.axis_index("mp")
        self.p = lax.rem(self.me, 4)
        self.a = self.me // 4
        x = lax.rem(self.p, 2)
        y = self.p // 2
        dx = 1 - 2 * x
        dy = 2 - 4 * y
        d_first = dx + self.core * (dy - dx)
        d_second = dy + self.core * (dx - dy)
        self.p_first = self.p + d_first
        self.p_second = self.p + d_second
        self.p_both = self.p + dx + dy
        self.first = {"blk": self.me + d_first}
        self.second = {"blk": self.me + d_second}
        self.sibling = {"mp": 1 - self.core}
        self.in_plane = 2 * self.p + self.core

    def group(self, level):
        return (self.a // 2**level) * 2**level

    def other_group(self, level):
        bit = lax.rem(self.a // 2**level, 2)
        return self.group(level) + (1 - 2 * bit) * 2**level

    def partner(self, level):
        bit = lax.rem(self.a // 2**level, 2)
        return {"blk": self.me + (1 - 2 * bit) * 2**level * 4}

    def partners(self):
        near = [self.partner(level) for level in range(self.levels)]
        return near + [self.first, self.second, self.sibling]

    def plane_mate(self, step):
        other = lax.rem(self.in_plane + step, 8)
        return {"blk": self.me - self.p + other // 2, "mp": lax.rem(other, 2)}

    def line_mate(self, step):
        return {"blk": self.me + 4 * (lax.rem(self.a + step, self.long) - self.a)}

    def mates(self):
        return [self.plane_mate(step) for step in range(1, 8)] + [
            self.line_mate(step) for step in range(1, self.long)
        ]


def enter(partners):
    barrier = pltpu.get_barrier_semaphore()
    for device in partners:
        pl.semaphore_signal(barrier, inc=1, device_id=device, device_id_type=MESH)
    pl.semaphore_wait(barrier, len(partners))


class Copies:
    def __init__(self, send, recv):
        self.send, self.recv, self.count, self.open = send, recv, 0, []

    def remote(self, src, dst, device):
        index = self.count
        self.count += 1
        copy = pltpu.make_async_remote_copy(
            src_ref=src,
            dst_ref=dst,
            send_sem=self.send.at[index],
            recv_sem=self.recv.at[index],
            device_id=device,
            device_id_type=MESH,
        )
        copy.start()
        self.open.append(copy)
        return copy

    def left(self, copy):
        copy.wait_send()
        self.open = [member for member in self.open if member is not copy]

    def finish(self):
        for copy in self.open:
            copy.wait_send()
        self.open = []


class Moves:
    def __init__(self, semaphores):
        self.semaphores, self.count, self.open = semaphores, 0, {}

    def start(self, name, src, dst):
        copy = pltpu.make_async_copy(src, dst, self.semaphores.at[self.count])
        self.count += 1
        copy.start()
        self.open[name] = copy

    def need(self, *names):
        for name in names:
            if name in self.open:
                self.open.pop(name).wait()

    def finish(self):
        self.need(*list(self.open))


def dot(left, right, dims=((1,), (0,))):
    return lax.dot_general(left, right, (dims, ((), ())), preferred_element_type=F32)


NN = ((1,), (0,))
NT = ((1,), (1,))


LINK_BYTES = 1e5
DELAY = 1.5
BACKLOG = 2.0


class Pump:
    def __init__(self, gate, ahead):
        self.now = 0.0
        self.free = {}
        self.flying = []
        self.count = 0
        self.pending = []
        self.gate, self.ahead = gate, ahead

    def _resume(self, chain):
        try:
            loads, after = next(chain)
        except StopIteration:
            return
        for link, size in loads.items():
            self.free[link] = max(self.free.get(link, 0.0), self.now) + size / LINK_BYTES
        self.count += 1
        end = max(self.free[link] for link in loads)
        self.flying.append((end + DELAY, self.count, chain, after))

    def _ready(self, entry):
        return max(entry[0], self.free.get(entry[3], 0.0) - BACKLOG)

    def _start(self):
        while self.pending and self.free.get(self.gate, 0.0) <= self.now + self.ahead:
            self._resume(self.pending.pop(0))

    def _next(self):
        soonest = min(self.flying, key=lambda entry: (self._ready(entry), entry[1]))
        self.flying = [entry for entry in self.flying if entry is not soonest]
        self.now = max(self.now, self._ready(soonest))
        self._resume(soonest[2])
        self._start()

    def add(self, *chains):
        self.pending.extend(chains)
        self._start()

    def work(self, spent):
        end = self.now + spent
        while self.flying and min(self._ready(entry) for entry in self.flying) <= end:
            self._next()
        self.now = max(self.now, end)
        self._start()

    def until(self, chain):
        busy = lambda: any(entry[2] is chain for entry in self.flying)
        while busy() or any(member is chain for member in self.pending):
            if not self.flying:
                self.now = max(self.now, self.free.get(self.gate, 0.0) - self.ahead)
                self._start()
            else:
                self._next()

    def drain(self):
        while self.flying or self.pending:
            if not self.flying:
                self.now = max(self.now, self.free.get(self.gate, 0.0) - self.ahead)
                self._start()
            else:
                self._next()


def bytes_of(ref):
    size = 2 if ref.dtype == BF else 4
    return size * int(np.prod(ref.shape))


EVERY = slice(None)


class View:
    def __init__(self, ref, *lead, columns=slice(None)):
        self.ref, self.lead, self.columns = ref, lead, columns

    def _index(self, index):
        index = self.lead + index
        return index + (EVERY,) * (len(self.ref.shape) - 1 - len(index)) + (self.columns,)

    def at(self, *index):
        return self.ref.at[self._index(index)]

    def get(self, *index):
        return self.ref[self._index(index)]

    def put(self, value, *index):
        self.ref[self._index(index)] = value.astype(self.ref.dtype)


def line_load(level, size):
    return {"ends": size} if level == 0 else {"ends": 2**level * size, "middle": 4**level * size}


def gather_chain(place, copies, slot, plane_first=False):
    unit = 2.0 * bytes_of(slot(0, 0))

    def plane(a, weight, after):
        one = copies.remote(slot(a, place.p), slot(a, place.p), place.first)
        two = copies.remote(slot(a, place.p), slot(a, place.p), place.second)
        yield {"xy": unit * weight}, "xy"
        two.wait_recv()
        three = copies.remote(slot(a, place.p_second), slot(a, place.p_second), place.first)
        yield {"xy": unit * weight / 2}, after
        one.wait_recv()
        three.wait_recv()

    def line(p, weight, after):
        for level in range(place.levels):
            zs = place.a if level == 0 else pl.ds(place.group(level), 2**level)
            sent = copies.remote(slot(zs, p), slot(zs, p), place.partner(level))
            yield line_load(level, unit * weight), "middle" if level + 1 < place.levels else after
            sent.wait_recv()

    if plane_first:
        yield from plane(place.a, 1, "ends")
        yield from line(EVERY, 4, None)
    else:
        yield from line(place.p, 1, "xy")
        yield from plane(EVERY, place.long, None)


def add_up(*terms):
    total = terms[0].astype(F32)
    for term in terms[1:]:
        total = total + term.astype(F32)
    return total


def scatter_chain(place, copies, grads, two, one, total, zs, out):
    long = place.long
    unit = 2.0 * bytes_of(grads.at(0, 0))
    far = copies.remote(grads.at(EVERY, place.p_both), two.at(1), place.first)
    near = copies.remote(grads.at(EVERY, place.p_first), two.at(0), place.first)
    yield {"xy": unit * long}, "xy"
    far.wait_recv()

    for z in range(long):
        total.put(add_up(grads.get(z, place.p_second), two.get(1, z)), z)

    last = copies.remote(total.at(), one.at(), place.second)
    yield {"xy": unit * long / 2}, "middle"
    near.wait_recv()
    last.wait_recv()
    copies.left(last)
    sent = []

    for z in range(long):
        total.put(add_up(grads.get(z, place.p), two.get(0, z), one.get(z)), z)

    for level in reversed(range(place.levels)):
        away = pl.ds(place.other_group(level), 2**level)
        landing = pl.ds(2**level - 1, 2**level)
        copy = copies.remote(total.at(away), zs.at(landing), place.partner(level))
        sent.append(copy)
        yield line_load(level, unit), "ends" if level > 0 else None
        copy.wait_recv()
        if level == 0:
            out.put(add_up(total.get(place.a), zs.get(0)))
        else:
            for z in range(2**level):
                mine = place.group(level) + z
                total.put(add_up(total.get(mine), zs.get(2**level - 1 + z)), mine)
    for copy in sent:
        copies.left(copy)


def scatter_line_first(place, copies, grads, two, one, total, zs, out):
    unit = 2.0 * bytes_of(grads.at(0, 0))
    top = place.levels - 1
    local = lambda z: lax.rem(z, 2**top)
    for level in reversed(range(place.levels)):
        source, at = (grads, lambda z: z) if level == top else (total, local)
        away = pl.ds(at(place.other_group(level)), 2**level)
        landing = pl.ds(2**level - 1, 2**level)
        copy = copies.remote(source.at(away), zs.at(landing), place.partner(level))
        yield line_load(level, 4 * unit), "ends" if level > 0 else "xy"
        copy.wait_recv()

        for z in range(2**level):
            mine = place.group(level) + z
            for p in range(4):
                total.put(
                    add_up(source.get(at(mine), p), zs.get(2**level - 1 + z, p)), local(mine), p
                )

    here = local(place.a)
    far = copies.remote(total.at(here, place.p_both), two.at(1), place.first)
    near = copies.remote(total.at(here, place.p_first), two.at(0), place.first)
    yield {"xy": unit}, "xy"
    far.wait_recv()
    total.put(add_up(total.get(here, place.p_second), two.get(1)), here, place.p_second)
    last = copies.remote(total.at(here, place.p_second), one.at(), place.second)
    yield {"xy": unit / 2}, None
    near.wait_recv()
    last.wait_recv()
    out.put(add_up(total.get(here, place.p), two.get(0), one.get()))


def sum_chain(place, copies, mine, plane, middle, line, out):
    plane[place.in_plane] = mine[...]
    sent = [
        copies.remote(mine, plane.at[place.in_plane], place.plane_mate(step)) for step in range(1, 8)
    ]
    yield {"xy": 0.0}, "middle"
    for copy in sent:
        copy.wait_recv()
    total = plane[0]
    for index in range(1, 8):
        total = total + plane[index]
    middle[...] = total
    line[place.a] = total
    sent = [
        copies.remote(middle, line.at[place.a], place.line_mate(step))
        for step in range(1, place.long)
    ]
    yield {"middle": 0.0}, None
    for copy in sent:
        copy.wait_recv()
    total = line[0]
    for index in range(1, place.long):
        total = total + line[index]
    out[...] = total


def norm_rows(values, gain):
    return values * lax.rsqrt(jnp.mean(values * values, axis=-1, keepdims=True) + norm_eps) * gain


def head_mask(which):
    lane = lax.broadcasted_iota(jnp.int32, (1, 128), 1)
    return jnp.where(lane // DH == which, 1.0, 0.0).astype(BF)


def make_eye(eye):
    row = lax.broadcasted_iota(jnp.int32, eye.shape, 0)
    column = lax.broadcasted_iota(jnp.int32, eye.shape, 1)
    eye[...] = jnp.where(row == column, 1.0, 0.0).astype(BF)


def turn(value, eye):
    parts = []
    for start in range(0, value.shape[1], 256):
        size = min(256, value.shape[1] - start)
        piece = value[:, start : start + size]
        parts.append(dot(eye[pl.ds(0, size), pl.ds(0, size)], piece, NT).astype(BF))
    return parts[0] if len(parts) == 1 else jnp.concatenate(parts, axis=0)


def lanes_at(start, pair):
    return pl.ds(start + pair * 128, 128)


CHUNK = 64


def bias_rows(bias, head, tiles, tile, key):
    blank = jnp.full((128, 128), masked_score, F32)
    away = [2 * tile - key, 2 * tile + 1 - key]
    return jnp.concatenate(
        [bias[head * tiles + each] if each >= 0 else blank for each in away], axis=1
    )


def grouped(chunk):
    return chunk.reshape(chunk.shape[0] // 8, 8, chunk.shape[1])


def eight_rows(row):
    return jnp.broadcast_to(row, (8, row.shape[1]))[None]


def softmax_chunks(load, chunks, low_out):
    top = None
    for index in range(chunks):
        most = jnp.max(grouped(load(index)), axis=0)
        top = most if top is None else jnp.maximum(top, most)
    top = jnp.max(top, axis=0, keepdims=True)
    wide_top = eight_rows(top)
    total = None
    for index in range(chunks):
        shifted = jnp.exp(grouped(load(index)) - wide_top)
        part = jnp.sum(shifted, axis=0)
        total = part if total is None else total + part
        low_out(index, shifted.reshape(CHUNK, shifted.shape[2]).astype(BF))
    total = jnp.sum(total, axis=0, keepdims=True)
    return (total, top + jnp.log(total))


def back_chunk(scores, dprobs, log_total, inner):
    probs = jnp.exp(grouped(scores) - log_total)
    dscores = probs * (grouped(dprobs) - inner)
    return (probs.reshape(scores.shape).astype(BF), dscores.reshape(scores.shape).astype(BF))


def self_forward(pair, qkv, bias, o1, o1_turned, lse, eye, scores, low_probs, between):
    width = o1.shape[1]
    tiles = qkv.shape[0] // 128
    values_turned = turn(qkv[:, lanes_at(2 * width, pair)], eye)
    for tile in range(tiles // 2):
        rows, seen = pl.ds(tile * 256, 256), (tile + 1) * 256
        query = qkv[rows, lanes_at(0, pair)]
        key = qkv[pl.ds(0, seen), lanes_at(width, pair)]
        made = []
        for which in range(2):
            head = 2 * pair + which
            scores[which, pl.ds(0, seen), :] = dot(key, query * head_mask(which), NT)

            def load(index):
                block = bias_rows(bias, head, tiles, tile, index // 2)
                at = (index % 2) * CHUNK
                return scores[which, pl.ds(index * CHUNK, CHUNK), :] + block[at : at + CHUNK]

            def low_out(index, value):
                low_probs[which, pl.ds(index * CHUNK, CHUNK), :] = value

            total, log_total = softmax_chunks(load, seen // CHUNK, low_out)
            lse[pl.ds(head, 1), rows] = log_total
            value = values_turned[which * DH : (which + 1) * DH, :seen]
            made.append(dot(value, low_probs[which, pl.ds(0, seen), :]) * (1.0 / total))
        made = jnp.concatenate(made, axis=0)
        o1_turned[lanes_at(0, pair), rows] = made
        o1[rows, lanes_at(0, pair)] = turn(made.astype(BF), eye)
        between()


def inner_rows(pair, which, o_turned, do_turned):
    here = pl.ds(pair * 128 + which * DH, DH)
    upstream = do_turned[which * DH : (which + 1) * DH, :].astype(F32)
    return eight_rows(jnp.sum(o_turned[here, :] * upstream, axis=0, keepdims=True))


def self_backward(
    pair, qkv, bias, lse, o1_turned, do1, dqkv, buckets, bias_total, eye,
    scores, dprobs, low_probs, low_dscores, between,
):
    width = do1.shape[1]
    length = qkv.shape[0]
    tiles = length // 128
    keys_turned = turn(qkv[:, lanes_at(width, pair)], eye)
    do_turned = turn(do1[:, lanes_at(0, pair)], eye)
    queries, upstreams = [], []
    for tile in range(tiles // 2):
        rows, seen = pl.ds(tile * 256, 256), (tile + 1) * 256
        query = qkv[rows, lanes_at(0, pair)]
        key = qkv[pl.ds(0, seen), lanes_at(width, pair)]
        value = qkv[pl.ds(0, seen), lanes_at(2 * width, pair)]
        upstream = do1[rows, lanes_at(0, pair)]
        made = []
        for which in range(2):
            head = 2 * pair + which
            at = pl.ds((2 * tile + which) * 256, 256)
            queries.append(query * head_mask(which))
            upstreams.append(upstream * head_mask(which))
            inner = inner_rows(pair, which, o1_turned.at[:, rows], do_turned[:, tile * 256 : seen])
            scores[which, pl.ds(0, seen), :] = dot(key, queries[-1], NT)
            dprobs[which, pl.ds(0, seen), :] = dot(value, upstreams[-1], NT)
            log_total = eight_rows(lse[pl.ds(head, 1), rows])
            for index in range(seen // CHUNK):
                here = pl.ds(index * CHUNK, CHUNK)
                block = bias_rows(bias, head, tiles, tile, index // 2)
                start = (index % 2) * CHUNK
                value_here = scores[which, here, :] + block[start : start + CHUNK]
                low_probs[here, at], low_dscores[here, at] = back_chunk(
                    value_here, dprobs[which, here, :], log_total, inner
                )
            made.append(
                dot(keys_turned[which * DH : (which + 1) * DH, :seen], low_dscores[pl.ds(0, seen), at])
            )
        dqkv[rows, lanes_at(0, pair)] = turn(jnp.concatenate(made, axis=0).astype(BF), eye)
        between()
    queries = jnp.concatenate(queries, axis=0)
    upstreams = jnp.concatenate(upstreams, axis=0)
    for tile in range(tiles // 2):
        rows, later = pl.ds(tile * 256, 256), pl.ds(tile * 512, 2 * length - tile * 512)
        dkey = dot(low_dscores[rows, later], queries[tile * 512 :])
        dqkv[rows, lanes_at(width, pair)] = dkey.astype(BF)
        dvalue = dot(low_probs[rows, later], upstreams[tile * 512 :])
        dqkv[rows, lanes_at(2 * width, pair)] = dvalue.astype(BF)
    for which in range(2):
        total = jnp.zeros((8, 128), F32)
        for away in range(tiles):
            summed = None
            for key in range(tiles - away):
                query = key + away
                start = (2 * (query // 2) + which) * 256 + (query % 2) * 128
                block = low_dscores[pl.ds(key * 128, 128), pl.ds(start, 128)].astype(F32)
                summed = block if summed is None else summed + block
            total = total + lax.dot_general(
                diagonal_sums(summed), buckets[away].astype(F32), (NN, ((), ())), precision=HIGHEST,
                preferred_element_type=F32,
            )
        row = lax.broadcasted_iota(jnp.int32, (8, 128), 0)
        bias_total[...] += jnp.where(row == 2 * pair + which, total, 0.0)


def diagonal_sums(tile):
    wide = jnp.concatenate([tile, jnp.zeros_like(tile)], axis=1)
    turned = wide[0:8]
    for group in range(1, 16):
        turned = turned + pltpu.roll(wide[8 * group : 8 * group + 8], 256 - 8 * group, 1)
    place_in = lax.broadcasted_iota(jnp.int32, (8, 256), 0)
    for bit in (1, 2, 4):
        moved = pltpu.roll(turned, 256 - bit, 1)
        turned = jnp.where(lax.rem(place_in // bit, 2) == 1, moved, turned)
    return jnp.broadcast_to(jnp.sum(turned, axis=0, keepdims=True), (8, 256))


def lane_row(index):
    lane = lax.broadcasted_iota(jnp.int32, (1, 128), 1)
    return jnp.where(lane == index, 1.0, 0.0).astype(BF)


def with_mask(key, mask, which):
    spot = lane_row((1 - which) * DH)
    return key * (1 - spot) + mask * spot


def with_one(query, which):
    return query * head_mask(which) + lane_row((1 - which) * DH)


def cross_forward(pair, q2, kc, vc, mask, o2, o2_turned, lse, eye, scores, low_probs, between):
    values_turned = turn(vc[:, lanes_at(0, pair)], eye)
    key = kc[:, lanes_at(0, pair)]
    keys = [with_mask(key, mask[...], which) for which in range(2)]
    for tile in range(q2.shape[0] // 256):
        rows = pl.ds(tile * 256, 256)
        query = q2[rows, lanes_at(0, pair)]
        made = []
        for which in range(2):
            scores[which] = dot(keys[which], with_one(query, which), NT)

            def load(index):
                return scores[which, pl.ds(index * CHUNK, CHUNK), :]

            def low_out(index, value):
                low_probs[which, pl.ds(index * CHUNK, CHUNK), :] = value

            total, log_total = softmax_chunks(load, key.shape[0] // CHUNK, low_out)
            lse[pl.ds(2 * pair + which, 1), rows] = log_total
            value = values_turned[which * DH : (which + 1) * DH, :]
            made.append(dot(value, low_probs[which]) * (1.0 / total))
        made = jnp.concatenate(made, axis=0)
        o2_turned[lanes_at(0, pair), rows] = made
        o2[rows, lanes_at(0, pair)] = turn(made.astype(BF), eye)
        between()


def cross_backward(
    pair, q2, kc, vc, mask, lse, o2_turned, do2, dq2, dkc, dvc, eye,
    scores, dprobs, low_probs, low_dscores, between,
):
    key, value = kc[:, lanes_at(0, pair)], vc[:, lanes_at(0, pair)]
    keys = [with_mask(key, mask[...], which) for which in range(2)]
    keys_turned = turn(key, eye)
    do_turned = turn(do2[:, lanes_at(0, pair)], eye)
    queries, upstreams = [], []
    for tile in range(q2.shape[0] // 256):
        rows = pl.ds(tile * 256, 256)
        query, upstream = q2[rows, lanes_at(0, pair)], do2[rows, lanes_at(0, pair)]
        made = []
        for which in range(2):
            at = pl.ds((2 * tile + which) * 256, 256)
            queries.append(query * head_mask(which))
            upstreams.append(upstream * head_mask(which))
            inner = inner_rows(
                pair, which, o2_turned.at[:, rows], do_turned[:, tile * 256 : (tile + 1) * 256]
            )
            scores[which] = dot(keys[which], with_one(query, which), NT)
            dprobs[which] = dot(value, upstreams[-1], NT)
            log_total = eight_rows(lse[pl.ds(2 * pair + which, 1), rows])
            for index in range(key.shape[0] // CHUNK):
                here = pl.ds(index * CHUNK, CHUNK)
                low_probs[here, at], low_dscores[here, at] = back_chunk(
                    scores[which, here, :], dprobs[which, here, :], log_total, inner
                )
            made.append(dot(keys_turned[which * DH : (which + 1) * DH, :], low_dscores[:, at]))
        dq2[rows, lanes_at(0, pair)] = turn(jnp.concatenate(made, axis=0).astype(BF), eye)
        between()
    dkc[:, lanes_at(0, pair)] = dot(low_dscores[...], jnp.concatenate(queries, axis=0)).astype(BF)
    dvc[:, lanes_at(0, pair)] = dot(low_probs[...], jnp.concatenate(upstreams, axis=0)).astype(BF)


def row_tiles(length):
    def run(step):
        for tile in range(length // 64):
            step(tile)

    return run


def rows_of(tile):
    return pl.ds(tile * 64, 64)


def back_through_norm(values, gain, upstream):
    scale = lax.rsqrt(jnp.mean(values * values, axis=-1, keepdims=True) + norm_eps)
    weighted = upstream * gain
    inner = jnp.mean(weighted * values, axis=-1, keepdims=True)
    return (
        scale * weighted - values * (scale * scale * scale * inner),
        jnp.sum(upstream * values * scale, axis=0, keepdims=True),
    )


def feed_tile(
    tile, h3, df, h3_turned, df_turned, feed, y_part, dn_part, g_feed, width,
    gate_up, dhidden, hidden, dpair,
):
    up_down = columns_of(feed, tile, 0, 2 * width)
    down = columns_of(feed, tile, 2 * width, width)
    gate_up[...] = dot(h3[...], up_down)
    dhidden[...] = dot(df[...], down)
    root = math.sqrt(2.0 / math.pi)

    @row_tiles(h3.shape[0])
    def _(index):
        rows = rows_of(index)
        gate, upper = gate_up[rows, pl.ds(0, width)], gate_up[rows, pl.ds(width, width)]
        upstream = dhidden[rows, :]
        square = gate * gate
        curve = jnp.tanh(gate * (root + root * 0.044715 * square))
        half = 0.5 + 0.5 * curve
        active = gate * half
        slope = half + 0.5 * gate * (1.0 - curve * curve) * (root + root * 3 * 0.044715 * square)
        hidden[rows, :] = (active * upper).astype(BF)
        dpair[rows, pl.ds(0, width)] = (upstream * upper * slope).astype(BF)
        dpair[rows, pl.ds(width, width)] = (upstream * active).astype(BF)

    y_now = dot(hidden[...], down, NT)
    dn_now = dot(dpair[...], up_down, NT)
    if tile == 0:
        y_part[...] = y_now
        dn_part[...] = dn_now
    else:
        y_part[...] += y_now
        dn_part[...] += dn_now
    put_columns(g_feed, tile, 0, dot(h3_turned[...], dpair[...]))
    put_columns(g_feed, tile, 2 * width, dot(df_turned[...], hidden[...]))


FEED_TILE = 256
PIECE = 768


def columns_of(ref, piece, start, count):
    value = ref[piece, :, :, :, pl.ds(start, count)]
    return value.reshape(value.shape[0] * value.shape[1] * value.shape[2], count)


def put_columns(ref, piece, start, value):
    ref[piece, :, :, :, pl.ds(start, value.shape[1])] = value.astype(ref.dtype).reshape(
        ref.shape[1:4] + (value.shape[1],)
    )


FRONT_OUT = (
    "near", "bias", "h1", "qkv", "lse1", "o1", "o1_turned", "x1", "h2", "q2", "enc_mine", "kc", "vc",
    "mask", "lse2", "o2", "o2_turned", "dx2", "g_feed", "layer_out", "stats",
)


def front_kernel(
    levels, slots,
    self_proj, self_out, cross_proj, cross_out, feed_in, feed_out, encoder, tok_own, grad_own,
    gains, bias_table, one_hot, blank, items, lengths, limit, *refs,
):
    outs = dict(zip(FRONT_OUT, refs))
    slot_of = refs[len(FRONT_OUT)]
    refs = refs[len(FRONT_OUT) + 1 :]
    kept = dict(zip(FRONT_OUT, refs))
    (
        near, bias, h1, qkv, lse1, o1, o1_turned, x1, h2, q2, enc_mine, kc, vc, mask, lse2, o2,
        o2_turned, dx2, g_feed, layer_out, stats,
    ) = refs[: len(FRONT_OUT)]
    (
        scores, low_probs, gate_up, dhidden, hidden, dpair, feed, enc, info, scalars, tok, grad,
        part_one, part_two, y_part, dn_part, got_one, got_two, got_y, got_dn, x2, h3, df, h3_turned,
        df_turned, eye, strips, send, recv, local,
    ) = refs[len(FRONT_OUT) :]
    place = Place(levels)
    enter(place.partners())
    copies, moves = Copies(send, recv), Moves(local)
    length, width = o1.shape
    half_rows = length // 2
    keep = lambda *names: [moves.start(name, kept[name], outs[name]) for name in names]
    tok_sent = copies.remote(tok_own, tok.at[place.core], place.sibling)

    def pack(piece, start, value):
        target = near if piece < near.shape[0] else feed
        at = pl.ds(start, value.shape[1])
        target[piece % near.shape[0], place.a, place.p, :, at] = value.astype(BF)

    for base, proj, out in ((0, self_proj, self_out), (2, cross_proj, cross_out)):
        pack(base, 0, proj[0])
        pack(base, width, proj[1])
        pack(base + 1, 0, proj[2])
        pack(base + 1, width, out[...])
    row = lax.broadcasted_iota(jnp.int32, (8, 128), 0)
    lane = lax.broadcasted_iota(jnp.int32, (8, 128), 1)
    known = jnp.zeros((8, 128), jnp.int32)
    per_chip = enc.shape[3]
    for index in range(per_chip):
        pair = jnp.where(lane == 0, items[index], jnp.where(lane == 1, lengths[index], 0))
        known = jnp.where(row == index, pair, known)
    info[place.a, place.p] = known
    half_cols = enc.shape[5]
    own_cols = pl.ds(pl.multiple_of(place.core * half_cols, half_cols), half_cols)
    enc[place.core, place.a, place.p] = encoder[:, own_cols].reshape(per_chip, KB, half_cols)
    for tile in range(feed.shape[0]):
        at = pl.ds(tile * FEED_TILE, FEED_TILE)
        pack(4 + tile, 0, feed_in[0, :, at])
        pack(4 + tile, FEED_TILE, feed_in[1, :, at])
        pack(4 + tile, 2 * FEED_TILE, feed_out[:, at])

    pump = Pump("ends", 1.5)

    def piece(index):
        target = near if index < near.shape[0] else feed
        return gather_chain(
            place, copies, lambda a, p: target.at[index % near.shape[0], a, p],
            plane_first=index == 3,
        )

    pieces = [piece(index) for index in range(near.shape[0] + feed.shape[0])]
    info_chain = gather_chain(place, copies, lambda a, p: info.at[a, p])
    enc_chain = gather_chain(place, copies, lambda a, p: enc.at[place.core, a, p])
    pump.add(info_chain, pieces[0], pieces[1], enc_chain, pieces[3], pieces[2], *pieces[4:])
    grad_sent = copies.remote(grad_own, grad.at[place.core], place.sibling)
    tok[place.core] = tok_own[...]
    grad[place.core] = grad_own[...]
    lse1[...] = jnp.zeros_like(lse1)
    lse2[...] = jnp.zeros_like(lse2)
    make_eye(eye)
    heads = width // DH
    strips[pl.ds(0, bias_table.shape[0]), :] = blank[...] + lax.dot_general(
        bias_table[...], one_hot[...], (NN, ((), ())), precision=HIGHEST, preferred_element_type=F32
    )
    tiles = length // 128
    for head in range(heads):
        for tile in range(tiles):
            strip = strips[pl.ds(place.core * heads + head, 1), pl.ds(tile * 256, 256)]
            rows = jnp.broadcast_to(strip, (128, 256))
            bias[head * tiles + tile] = pltpu.roll(rows, 0, 1, stride=1, stride_axis=0)[:, :128]
    keep("bias")
    pump.work(3.0)
    tok_sent.wait_recv()

    @row_tiles(length)
    def _(tile):
        part = tile // (half_rows // 64)
        values = tok[part, rows_of(tile - part * (half_rows // 64)), :].astype(F32)
        h1[rows_of(tile), :] = norm_rows(values, gains[0:1, :]).astype(BF)

    keep("h1")
    pump.work(2.0)
    pump.until(pieces[0])
    qkv[:, pl.ds(0, 2 * width)] = dot(h1[...], columns_of(near, 0, 0, 2 * width)).astype(BF)
    pump.work(2.0)
    pump.until(pieces[1])
    qkv[:, pl.ds(2 * width, width)] = dot(h1[...], columns_of(near, 1, 0, width)).astype(BF)
    keep("qkv")
    pump.work(1.0)
    for pair in range(width // 128):
        self_forward(
            pair, qkv, bias, o1, o1_turned, lse1, eye, scores, low_probs, lambda: pump.work(1.5)
        )
    keep("lse1", "o1", "o1_turned")
    part_one[...] = dot(o1[...], columns_of(near, 1, width, width), NT)
    one_sent = copies.remote(part_one, got_one, place.sibling)
    pump.work(1.0)
    pump.until(enc_chain)
    enc_sent = copies.remote(enc.at[place.core], enc.at[place.core], place.sibling)
    pump.until(info_chain)
    moves.start("info", info, scalars)
    pump.work(2.0)
    one_sent.wait_recv()

    @row_tiles(length)
    def _(tile):
        rows = rows_of(tile)
        part = tile // (half_rows // 64)
        values = tok[part, rows_of(tile - part * (half_rows // 64)), :].astype(F32)
        values = values + (part_one[rows, :] + got_one[rows, :])
        x1[rows, :] = values
        h2[rows, :] = norm_rows(values, gains[1:2, :]).astype(BF)

    keep("x1", "h2")
    moves.need("info")
    total_blocks = enc.shape[1] * 4 * per_chip

    def block_at(block):
        chip = block // per_chip
        return (chip // 4, lax.rem(chip, 4), lax.rem(block, per_chip))

    def look(block, carried):
        count, found, sizes = carried
        z, p, at = block_at(block)
        own = (scalars[z, p, at, 0] == place.me).astype(jnp.int32)
        slot_of[block] = own * count + (1 - own) * slots
        here = [own * (count == index).astype(jnp.int32) for index in range(slots)]
        found = tuple(known + each * block for known, each in zip(found, here))
        sizes = tuple(known + each * scalars[z, p, at, 1] for known, each in zip(sizes, here))
        return (count + own, found, sizes)

    nothing = (jnp.int32(0),) * slots
    _, found, sizes = lax.fori_loop(0, total_blocks, look, (jnp.int32(0), nothing, nothing))
    pump.work(3.0)
    pump.until(pieces[2])
    pump.until(pieces[3])
    keep("near")
    enc_sent.wait_recv()
    place_in = lax.broadcasted_iota(jnp.int32, (KB, 128), 0)
    for index in range(slots):
        here = pl.ds(index * KB, KB)
        z, p, at = block_at(found[index])
        for half in range(2):
            enc_mine[here, pl.ds(half * half_cols, half_cols)] = enc[half, z, p, at]
        mask[here, :] = jnp.where(place_in < sizes[index], 0.0, masked_score).astype(BF)
    keep("enc_mine", "mask")
    pump.work(1.0)
    q2[...] = dot(h2[...], columns_of(near, 2, 0, width)).astype(BF)
    kc[...] = dot(enc_mine[...], columns_of(near, 2, width, width)).astype(BF)
    vc[...] = dot(enc_mine[...], columns_of(near, 3, 0, width)).astype(BF)
    keep("q2", "kc", "vc")
    pump.work(4.0)
    for pair in range(width // 128):
        cross_forward(
            pair, q2, kc, vc, mask, o2, o2_turned, lse2, eye, scores, low_probs,
            lambda: pump.work(2.5),
        )
    keep("lse2", "o2", "o2_turned")
    part_two[...] = dot(o2[...], columns_of(near, 3, width, width), NT)
    two_sent = copies.remote(part_two, got_two, place.sibling)
    pump.work(1.0)
    grad_sent.wait_recv()
    top = limit[0]

    @row_tiles(length)
    def _(tile):
        part = tile // (half_rows // 64)
        rows = rows_of(tile)
        row = lax.broadcasted_iota(jnp.int32, (64, 1), 0) + tile * 64
        values = grad[part, rows_of(tile - part * (half_rows // 64)), :].astype(F32)
        df[rows, :] = jnp.where(row < top, values, 0.0).astype(BF)

    two_sent.wait_recv()

    @row_tiles(length)
    def _(tile):
        rows = rows_of(tile)
        values = x1[rows, :] + (part_two[rows, :] + got_two[rows, :])
        x2[rows, :] = values
        h3[rows, :] = norm_rows(values, gains[2:3, :]).astype(BF)

    h3_turned[...] = turn(h3[...], eye)
    df_turned[...] = turn(df[...], eye)
    pump.work(4.0)
    for tile in range(feed.shape[0]):
        pump.until(pieces[4 + tile])
        feed_tile(
            tile, h3, df, h3_turned, df_turned, feed, y_part, dn_part, g_feed,
            FEED_TILE, gate_up, dhidden, hidden, dpair,
        )
        moves.start(("g_feed", tile), g_feed.at[tile], outs["g_feed"].at[tile])
        pump.work(5.0)
    pump.drain()
    dn_sent = copies.remote(dn_part, got_dn, place.sibling)
    other_rows = pl.ds(pl.multiple_of((1 - place.core) * half_rows, half_rows), half_rows)
    y_sent = copies.remote(y_part.at[other_rows, :], got_y, place.sibling)
    dn_sent.wait_recv()
    stats[...] = jnp.zeros_like(stats)

    @row_tiles(length)
    def _(tile):
        rows = rows_of(tile)
        delta, gain = back_through_norm(
            x2[rows, :], gains[2:3, :], dn_part[rows, :] + got_dn[rows, :]
        )
        dx2[rows, :] = df[rows, :].astype(F32) + delta
        stats[0:1, :] += gain

    keep("dx2")
    y_sent.wait_recv()

    @row_tiles(half_rows)
    def _(tile):
        rows = rows_of(tile)
        start = pl.multiple_of(place.core * half_rows + tile * 64, 64)
        here = pl.ds(start, 64)
        values = x2[here, :] + (y_part[here, :] + got_y[rows, :])
        layer_out[rows, :] = values.astype(BF)
        row = lax.broadcasted_iota(jnp.int32, (64, 1), 0) + start
        stats[1:2, :] += jnp.sum(jnp.where(row < top, values * values, 0.0), axis=0, keepdims=True)

    keep("layer_out", "stats")
    moves.finish()
    copies.finish()


def front_shapes(blocks, slots, length, width, rows, pieces):
    long = blocks // 4
    heads = width // DH
    tiles = length // 128
    keys = slots * KB
    return {
        "near": ((pieces, long, 4, rows, PIECE), BF),
        "bias": ((heads * tiles, 128, 128), F32),
        "h1": ((length, D), BF),
        "qkv": ((length, 3 * width), BF),
        "lse1": ((8, length), F32),
        "o1": ((length, width), BF),
        "o1_turned": ((width, length), F32),
        "x1": ((length, D), F32),
        "h2": ((length, D), BF),
        "q2": ((length, width), BF),
        "enc_mine": ((keys, D), BF),
        "kc": ((keys, width), BF),
        "vc": ((keys, width), BF),
        "mask": ((keys, 128), BF),
        "lse2": ((8, length), F32),
        "o2": ((length, width), BF),
        "o2_turned": ((width, length), F32),
        "dx2": ((length, D), F32),
        "g_feed": ((pieces, long, 4, rows, PIECE), BF),
        "layer_out": ((length // 2, D), BF),
        "stats": ((8, D), F32),
    }


SMEM = pl.BlockSpec(memory_space=pltpu.SMEM)


def front(blocks, slots, shapes, operands, scalars, per_chip):
    levels = int(math.log2(blocks)) - 2
    long = blocks // 4
    length = shapes["h1"][0][0]
    pieces, rows = shapes["near"][0][0], shapes["near"][0][3]
    keys = slots * KB
    count = (2 * pieces + 2) * (levels + 3) + 8
    outs = tuple(jax.ShapeDtypeStruct(*shapes[name]) for name in FRONT_OUT)
    wide = pltpu.VMEM((length, D), F32)
    low = pltpu.VMEM((length, D), BF)
    return pl.pallas_call(
        functools.partial(front_kernel, levels, slots),
        out_shape=outs + (jax.ShapeDtypeStruct((blocks * per_chip,), jnp.int32),),
        in_specs=[VMEM] * len(operands) + [SMEM] * len(scalars),
        out_specs=(ANY,) * len(outs) + (SMEM,),
        scratch_shapes=[pltpu.VMEM(*shapes[name]) for name in FRONT_OUT]
        + [
            pltpu.VMEM((2, keys, 256), F32),
            pltpu.VMEM((2, keys, 256), BF),
            pltpu.VMEM((length, 2 * FEED_TILE), F32),
            pltpu.VMEM((length, FEED_TILE), F32),
            pltpu.VMEM((length, FEED_TILE), BF),
            pltpu.VMEM((length, 2 * FEED_TILE), BF),
            pltpu.VMEM(*shapes["near"]),
            pltpu.VMEM((2, long, 4, per_chip, KB, D // 2), BF),
            pltpu.VMEM((long, 4, 8, 128), jnp.int32),
            pltpu.SMEM((long, 4, 8, 128), jnp.int32),
            pltpu.VMEM((2, length // 2, D), BF),
            pltpu.VMEM((2, length // 2, D), BF),
            wide, wide, wide, wide, wide, wide,
            pltpu.VMEM((length // 2, D), F32),
            wide, wide, low, low,
            pltpu.VMEM((D, length), BF),
            pltpu.VMEM((D, length), BF),
            pltpu.VMEM((256, 256), BF),
            pltpu.VMEM((16, 256 * (length // 128)), F32),
            pltpu.SemaphoreType.DMA((count,)),
            pltpu.SemaphoreType.DMA((count,)),
            pltpu.SemaphoreType.DMA((len(FRONT_OUT) + pieces + 1,)),
        ],
        compiler_params=pltpu.CompilerParams(
            collective_id=0, has_side_effects=True, vmem_limit_bytes=int(63.4 * 2**20)
        ),
    )(*operands, *scalars)


BACK_IN = (
    "g_feed", "near", "dx2", "o2", "q2", "kc", "vc", "mask", "lse2", "o2_turned", "h2", "x1",
    "o1", "qkv", "bias", "lse1", "o1_turned", "h1", "stats",
)


def put_outer(ref, piece, start, left, right, eye):
    long, half = ref.shape[1] // 2, D // 2
    for index in range(2):
        turned = turn(left[:, pl.ds(index * half, half)].astype(BF), eye)
        value = dot(turned, right).astype(BF)
        value = value.reshape((long,) + ref.shape[2:4] + (value.shape[1],))
        ref[piece, pl.ds(long * index, long), :, :, pl.ds(start, value.shape[3])] = value


def put_rows(ref, left, right, dims, add=False):
    for start in range(0, ref.shape[0], 256):
        rows = pl.ds(start, 256)
        value = dot(left[rows, :].astype(BF), right, dims)
        ref[rows, :] = (ref[rows, :] + value if add else value).astype(ref.dtype)


def back_kernel(
    levels, slots,
    gains, tok_own, buckets, slot_of, limit, enc_kept, *refs,
):
    sources = dict(zip(BACK_IN, refs))
    grad_out, decoder_grad, encoder_grad, sums, squares = refs[len(BACK_IN) : len(BACK_IN) + 5]
    refs = refs[len(BACK_IN) + 5 :]
    landed = dict(zip(BACK_IN, refs))
    (
        g_feed, near, dx2, o2, q2, kc, vc, mask, lse2, o2_turned, h2, x1, o1, qkv, bias, lse1,
        o1_turned, h1, stats,
    ) = refs[: len(BACK_IN)]
    (
        g_near, two, one, total, zs, line_two, line_one, line_total, line_zs, spread, e_two, e_one,
        e_total, e_zs, do, dq, dkc, dvc, dqkv, e_all, e_got, part, got_dn, got_half,
        bias_total, small, small_plane, small_middle, small_line, last, last_plane, last_middle,
        last_line, eye, scores, dprobs, low_probs, low_dscores, free, send, recv, local,
    ) = refs[len(BACK_IN) :]
    place = Place(levels)
    copies, moves = Copies(send, recv), Moves(local)
    near_pieces = near.shape[0]
    for name in BACK_IN:
        moves.start(name, sources[name], landed[name])
    enter(place.mates())
    pump = Pump("xy", 4.0)
    length, width = o1.shape
    half_rows = length // 2
    top = limit[0]
    half_cols = e_all.shape[3]

    def piece(index):
        source = View(g_near if index < near_pieces else g_feed, index % near_pieces)
        out = View(grad_out, index)
        if index == near_pieces:
            scratch = [View(ref) for ref in (line_two, line_one, line_total, line_zs)]
            return scatter_line_first(place, copies, source, *scratch, out)
        at = spot[index]
        scratch = [View(ref, at) for ref in (two, one, total, zs)]
        return scatter_chain(place, copies, source, *scratch, out)

    def half_piece(index, start):
        columns = pl.ds(start, width)
        scratch = [View(ref, spot[index], columns=columns) for ref in (two, one, total, zs)]
        return scatter_chain(
            place, copies, View(g_near, index, columns=columns), *scratch,
            View(grad_out, index, columns=columns),
        )

    spot = {5: 0, 6: 1, 7: 2, 2: 3, 3: 4, 0: 0, 1: 1}

    moves.need("g_feed")
    feed_chains = [piece(index) for index in range(near_pieces, near_pieces + g_feed.shape[0])]
    pump.add(*feed_chains)
    make_eye(eye)
    moves.need("near", "dx2", "o2")
    put_rows(do, dx2, columns_of(near, 3, width, width), NN)
    put_outer(g_near, 3, width, dx2, o2[...], eye)
    pump.work(2.5)
    moves.need("q2", "kc", "vc", "mask", "lse2", "o2_turned")
    for pair in range(width // 128):
        cross_backward(
            pair, q2, kc, vc, mask, lse2, o2_turned, do, dq, dkc, dvc, eye,
            scores, dprobs, low_probs, low_dscores, lambda: pump.work(4.0),
        )
    enc_mine = low_probs.at[:, pl.ds(0, D)]
    moves.start("enc_mine", enc_kept, enc_mine)
    pump.work(2.0)
    put_rows(part, dq, columns_of(near, 2, 0, width), NT)
    dn_sent = copies.remote(part, got_dn, place.sibling)
    half_long = near.shape[1] // 2
    for index in range(2):
        weights = [
            near[piece, half_long * index : half_long * (index + 1), :, :, pl.ds(start, width)]
            .reshape(half_cols, width)
            for piece, start in ((2, width), (3, 0))
        ]
        for first in range(0, slots, 6):
            keys = pl.ds(first * KB, 6 * KB)
            term = dot(dkc[keys, :], weights[0], NT) + dot(dvc[keys, :], weights[1], NT)
            e_all[index, pl.ds(first, 6)] = term.astype(BF).reshape(6, KB, half_cols)

    e_sent = copies.remote(
        e_all.at[1 - place.core, pl.ds(0, slots)], e_got, place.sibling
    )
    pump.work(2.0)
    moves.need("h2")
    put_outer(g_near, 2, 0, h2, dq[...], eye)
    moves.need("enc_mine")
    put_outer(g_near, 2, width, low_probs, dkc[...], eye)
    pump.work(1.5)
    put_outer(g_near, 3, 0, low_probs, dvc[...], eye)
    pump.work(1.5)
    pump.add(piece(2), piece(3))
    e_sent.wait_recv()

    for index in range(slots):
        own = e_all[place.core, index].astype(F32)
        e_all[place.core, index] = (own + e_got[index].astype(F32)).astype(BF)

    e_all[place.core, slots] = jnp.zeros((KB, half_cols), BF)
    per_chip = spread.shape[2] // KB
    for block in range(spread.shape[0] * 4 * per_chip):
        chip, at = block // per_chip, block % per_chip
        spread[chip // 4, chip % 4, pl.ds(at * KB, KB), :] = e_all[place.core, slot_of[block]]
    scratch = [View(ref) for ref in (spread, e_two, e_one, e_total, e_zs, encoder_grad)]
    pump.add(scatter_chain(place, copies, *scratch))
    moves.need("x1")
    dn_sent.wait_recv()
    sums[...] = jnp.zeros_like(sums)
    bias_total[...] = jnp.zeros_like(bias_total)

    @row_tiles(length)
    def _(tile):
        rows = rows_of(tile)
        delta, gain = back_through_norm(x1[rows, :], gains[1:2, :], part[rows, :] + got_dn[rows, :])
        dx2[rows, :] = dx2[rows, :] + delta
        sums[1:2, :] += 0.5 * gain

    pump.work(4.0)
    moves.need(*BACK_IN)
    put_rows(do, dx2, columns_of(near, 1, width, width), NN)
    put_outer(g_near, 1, width, dx2, o1[...], eye)
    pump.work(2.5)
    pump.until(feed_chains[1])
    pump.until(feed_chains[2])
    writers = [place.first, place.second] + [place.partner(level) for level in range(levels)]
    for device in writers:
        pl.semaphore_signal(free, inc=1, device_id=device, device_id_type=MESH)
    pl.semaphore_wait(free, len(writers))
    pump.add(half_piece(1, width))
    for pair in range(width // 128):
        self_backward(
            pair, qkv, bias, lse1, o1_turned, do, dqkv, buckets, bias_total, eye,
            scores, dprobs, low_probs, low_dscores, lambda: pump.work(2.5),
        )
    pump.work(1.0)
    put_outer(g_near, 0, 0, h1, dqkv[:, pl.ds(0, 2 * width)], eye)
    pump.add(half_piece(0, 0), half_piece(0, width))
    pump.work(1.0)
    put_outer(g_near, 1, 0, h1, dqkv[:, pl.ds(2 * width, width)], eye)
    pump.add(half_piece(1, 0))
    copies.left(dn_sent)
    wide = pl.ds(0, 2 * width), pl.ds(2 * width, width)
    for index, columns in enumerate(wide):
        weights = columns_of(near, index, 0, columns.size)
        put_rows(part, dqkv.at[:, columns], weights, NT, add=index > 0)
    own_rows = pl.multiple_of(place.core * half_rows, half_rows)
    other_rows = pl.ds(pl.multiple_of((1 - place.core) * half_rows, half_rows), half_rows)
    half_sent = copies.remote(part.at[other_rows, :], got_half, place.sibling)
    pump.work(3.0)
    half_sent.wait_recv()
    sums[2:3, :] = 0.5 * stats[0:1, :]
    sums[3:4, :] = stats[1:2, :]

    @row_tiles(half_rows)
    def _(tile):
        rows = rows_of(tile)
        start = pl.multiple_of(own_rows + tile * 64, 64)
        here = pl.ds(start, 64)
        values = tok_own[rows, :].astype(F32)
        delta, gain = back_through_norm(values, gains[0:1, :], part[here, :] + got_half[rows, :])
        result = dx2[here, :] + delta
        decoder_grad[rows, :] = result
        row = lax.broadcasted_iota(jnp.int32, (64, 1), 0) + start
        sums[0:1, :] += gain
        sums[4:5, :] += jnp.sum(jnp.where(row < top, result * result, 0.0), axis=0, keepdims=True)
        sums[5:6, :] += jnp.sum(jnp.where(row < top, 1.0, 0.0), axis=0, keepdims=True) * jnp.ones((1, D), F32)

    rows_bias = bias_total[...]
    for index in range(2):
        keep = jnp.where(place.core == index, 1.0, 0.0)
        sums[pl.ds(8 + 8 * index, 8), pl.ds(0, 128)] = rows_bias * keep
    small[...] = sums[...]
    pump.add(sum_chain(place, copies, small, small_plane, small_middle, small_line, sums))
    pump.drain()
    square = jnp.zeros((8, 128), F32)
    for index in range(grad_out.shape[0]):
        for start in range(0, PIECE, 128):
            tile = grad_out[index, :, pl.ds(start, 128)]
            tile = tile * tile
            for row in range(0, tile.shape[0], 8):
                square = square + tile[row : row + 8]
    last[...] = square
    pump.add(sum_chain(place, copies, last, last_plane, last_middle, last_line, squares))
    pump.drain()
    copies.finish()


def back(blocks, slots, shapes, made, tok_own, gains, limit, buckets, key_rows):
    levels = int(math.log2(blocks)) - 2
    long = blocks // 4
    pieces, rows = shapes["near"][0][0], shapes["near"][0][3]
    length, width = shapes["o1"][0]
    keys = slots * KB
    half = D // 2
    by_name = dict(zip(FRONT_OUT, made))
    count = (2 * pieces + 3) * (levels + 3) + 3 + 2 * (7 + long - 1)
    shape = lambda *dims: jax.ShapeDtypeStruct(dims, F32)
    outs = (
        shape(2 * pieces, rows, PIECE),
        shape(length // 2, D),
        shape(key_rows, half),
        shape(24, D),
        shape(8, 128),
    )
    steps = 2**levels - 1
    usual = 5
    block = (rows, PIECE)
    enc_block = (key_rows, half)
    sizes = [shapes["near"]]
    sizes += [((usual,) + lead + block, BF) for lead in ((2, long), (long,), (long,), (steps,))]
    sizes += [(lead + block, BF) for lead in ((2,), (), (long // 2, 4), (steps, 4))]
    sizes += [
        (lead + enc_block, BF) for lead in ((long, 4), (2, long), (long,), (long,), (steps,))
    ]
    sizes += [
        ((length, width), BF), ((length, width), BF), ((keys, width), BF), ((keys, width), BF),
        ((length, 3 * width), BF), ((2, slots + 1, KB, half), BF),
        ((slots, KB, half), BF), ((length, D), F32), ((length, D), F32), ((length // 2, D), F32),
        ((8, 128), F32),
    ]
    for member in ((24, D), (8, 128)):
        sizes += [(lead + member, F32) for lead in ((), (8,), (), (long,))]
    sizes += [
        ((256, 256), BF), ((2, keys, 256), F32), ((2, keys, 256), F32), ((keys, 2 * length), BF),
        ((keys, 2 * length), BF),
    ]
    return pl.pallas_call(
        functools.partial(back_kernel, levels, slots),
        out_shape=outs,
        in_specs=[VMEM, VMEM, VMEM, SMEM, SMEM] + [ANY] * (len(BACK_IN) + 1),
        out_specs=(VMEM,) * 5,
        scratch_shapes=[pltpu.VMEM(*shapes[name]) for name in BACK_IN]
        + [pltpu.VMEM(*size) for size in sizes]
        + [
            pltpu.SemaphoreType.REGULAR,
            pltpu.SemaphoreType.DMA((count,)),
            pltpu.SemaphoreType.DMA((count,)),
            pltpu.SemaphoreType.DMA((len(BACK_IN) + 1,)),
        ],
        compiler_params=pltpu.CompilerParams(
            collective_id=1, has_side_effects=True, vmem_limit_bytes=int(63.4 * 2**20)
        ),
    )(
        gains, tok_own, buckets, made[-1], limit, by_name["enc_mine"],
        *(by_name[name] for name in BACK_IN),
    )


def adam_kernel(grads, sums, squares, *refs):
    params, firsts, seconds, passed = refs[:8], refs[8:16], refs[16:24], refs[24:27]
    news, new_firsts, new_seconds = refs[27:35], refs[35:43], refs[43:51]
    norm_ref, rms_ref = refs[51:53]
    for index in range(3):
        refs[53 + index][...] = passed[index][...]
    width = params[0].shape[2]
    heads, known = params[7].shape
    gains = sums[0:3, :]
    by_head = jnp.concatenate(
        [sums[8 : 8 + heads // 2, 0:128], sums[16 : 16 + heads // 2, 0:128]], axis=0
    )[:, :known]
    whole = lambda value: jnp.sum(jnp.sum(value, axis=1, keepdims=True), axis=0, keepdims=True)
    norm = jnp.sqrt(whole(squares[...]) + whole(gains * gains) + whole(by_head * by_head))
    factor = jnp.minimum(1.0, clip_limit / (norm + 1e-06))
    norm_ref[...] = norm
    counted = sums[5:6, 0:1] * D
    rms_ref[...] = jnp.concatenate(
        [jnp.sqrt(whole(sums[3:4, :]) / counted), jnp.sqrt(whole(sums[4:5, :]) / counted)], axis=1
    )

    def update(index, at, grad):
        decay = weight_decay if index < 6 else 0.0
        weight, moment, second = adamw(
            params[index][at], firsts[index][at], seconds[index][at], grad * factor, decay,
            learn_rates[index],
        )
        news[index][at] = weight
        new_firsts[index][at] = moment
        new_seconds[index][at] = second

    columns = lambda piece, start, count: grads[piece, :, pl.ds(start, count)]
    for index, base in ((0, 0), (2, 2)):
        update(index, (0,), columns(base, 0, width))
        update(index, (1,), columns(base, width, width))
        update(index, (2,), columns(base + 1, 0, width))
        update(index + 1, (slice(None),), columns(base + 1, width, width))
    for tile in range(params[5].shape[1] // FEED_TILE):
        at = pl.ds(tile * FEED_TILE, FEED_TILE)
        for part in range(2):
            update(4, (part, slice(None), at), columns(4 + tile, part * FEED_TILE, FEED_TILE))
        update(5, (slice(None), at), columns(4 + tile, 2 * FEED_TILE, FEED_TILE))
    update(6, (slice(None),), gains)
    update(7, (slice(None),), by_head)


TURNED = (1, 3, 5, 7)


def turned_views(group):
    return [member.T if index in TURNED else member for index, member in enumerate(group)]


def adam(grads, sums, squares, params, firsts, seconds, passed):
    params, firsts, seconds = (turned_views(group) for group in (params, firsts, seconds))
    same = [jax.ShapeDtypeStruct(member.shape, F32) for member in params]
    outs = same * 3 + [jax.ShapeDtypeStruct((1, 1), F32), jax.ShapeDtypeStruct((1, 2), F32)]
    outs += [jax.ShapeDtypeStruct(member.shape, member.dtype) for member in passed]
    made = pl.pallas_call(
        adam_kernel,
        out_shape=tuple(outs),
        in_specs=[VMEM] * 30,
        out_specs=(VMEM,) * 29,
        compiler_params=pltpu.CompilerParams(vmem_limit_bytes=60 * 2**20),
    )(grads, sums, squares, *params, *firsts, *seconds, *passed)
    groups = [turned_views(made[start : start + 8]) for start in (0, 8, 16)]
    return (sum(groups, []), made[24], made[25], made[26:])


def fused(*args):
    (decoder_in, encoder_out, out_grad, block_items, block_lengths, target_lengths) = args[:6]
    params, firsts, seconds = args[6:14], args[14:22], args[22:30]
    norm_gains, position_bias = params[6:]
    blocks = lax.axis_size("blk")
    length = 2 * decoder_in.shape[0]
    key_rows = encoder_out.shape[0]
    width = params[0].shape[2]
    rows = params[0].shape[1]
    per_chip = key_rows // KB
    total_blocks = blocks * per_chip
    most = total_blocks - blocks * target_lengths.shape[0] + 1
    slots = -(-most // 6) * 6
    tiles = length // 128
    offsets = np.arange(256)
    steps = np.where(offsets < 128, offsets, offsets - 256)[None] + 128 * np.arange(tiles)[:, None]
    one_hot = np.eye(position_bias.shape[0], dtype=np.float32)[bucket_of(np.maximum(steps, 0))]
    one_hot = one_hot * (steps >= 0)[..., None]
    buckets = np.zeros((tiles, 256, 128), np.float32)
    buckets[:, :, : one_hot.shape[2]] = one_hot
    blank = np.where(steps >= 0, 0.0, masked_score).astype(np.float32).reshape(1, -1)
    shapes = front_shapes(blocks, slots, length, width, rows, 8 * width // PIECE)
    weights = turned_views(params)[:6]
    operands = weights + [
        encoder_out, decoder_in, out_grad, norm_gains, position_bias.T,
        jnp.asarray(one_hot.reshape(tiles * 256, -1).T), jnp.asarray(blank),
    ]
    scalars = [block_items, block_lengths, target_lengths]
    made = front(blocks, slots, shapes, operands, scalars, per_chip)
    grads, decoder_grad, encoder_grad, sums, squares = back(
        blocks, slots, shapes, made, decoder_in, norm_gains, target_lengths,
        jnp.asarray(buckets, BF), key_rows,
    )
    layer_out = made[FRONT_OUT.index("layer_out")]
    updated, norm, rms, passed = adam(
        grads, sums, squares, params, firsts, seconds, [layer_out, decoder_grad, encoder_grad]
    )
    return (*passed, *updated, norm.reshape(()), rms.reshape(2))


def plain_body(
    decoder_in,
    encoder_out,
    out_grad,
    block_items,
    block_lengths,
    target_lengths,
    self_proj,
    self_out,
    cross_proj,
    cross_out,
    feed_in,
    feed_out,
    norm_gains,
    position_bias,
    *moments,
):
    core = lax.axis_index("mp")
    rank = lax.axis_index("blk")
    blocks = lax.axis_size("blk")
    rows_own = decoder_in.shape[0]
    length = 2 * rows_own
    half = self_proj.shape[2]
    heads = half // DH
    hidden_half = feed_in.shape[2]
    key_rows = encoder_out.shape[0]

    params = [self_proj, self_out, cross_proj, cross_out, feed_in, feed_out]
    flat = []
    for value in params:
        if value.ndim == 3:
            flat.extend(value[index].astype(BF) for index in range(value.shape[0]))
        else:
            flat.append(value.astype(BF).T)
    shard = jnp.concatenate(flat, axis=1)
    edges = np.cumsum([0] + [member.shape[1] for member in flat]).tolist()
    places = jnp.arange(key_rows, dtype=jnp.int32)
    tags_own = jnp.where(
        places % KB < jnp.repeat(block_lengths, KB), jnp.repeat(block_items, KB), -1
    )
    encoder_half = lax.dynamic_slice_in_dim(encoder_out, core * (D // 2), D // 2, 1)
    weights = lax.all_gather(shard, "blk", axis=0, tiled=True)
    encoder = lax.all_gather(encoder_out, "blk", axis=0, tiled=True)
    tags = lax.all_gather(tags_own, "blk", axis=0, tiled=True)
    tokens = lax.all_gather(decoder_in, "mp")
    upstream = lax.all_gather(out_grad, "mp")
    tokens = tokens.reshape(length, D).astype(F32)
    limit = target_lengths[0]
    valid = (jnp.arange(length, dtype=jnp.int32) < limit).astype(F32)[:, None]
    dy = upstream.reshape(length, D).astype(F32) * valid
    w_q, w_k, w_v, w_so, c_q, c_k, c_v, w_co, f_g, f_u, f_d = (
        weights[:, edges[index] : edges[index + 1]] for index in range(11)
    )

    def both(term):
        pair = lax.all_gather(term, "mp")
        return pair[0] + pair[1]

    def dot(left, right, dims=((1,), (0,))):
        return lax.dot_general(left, right, (dims, ((), ())), preferred_element_type=F32)

    NT = ((1,), (1,))
    TN = ((0,), (0,))
    h1 = rms_norm(tokens, norm_gains[0]).astype(BF)
    q1, k1, v1 = (dot(h1, w).astype(BF).reshape(length, heads, DH) for w in (w_q, w_k, w_v))
    bias_here = lax.dynamic_slice_in_dim(position_bias, core * heads, heads, 1)
    spots = np.arange(length)
    buckets = bucket_of(np.maximum(spots, 0))
    by_distance = jnp.dot(
        jnp.asarray(np.eye(position_bias.shape[0], dtype=np.float32)[buckets]),
        bias_here,
        precision=HIGHEST,
    )
    tiles = length // 128
    offsets = np.arange(256)
    steps = np.where(offsets < 128, -offsets, 256 - offsets)[None] + 128 * np.arange(tiles)[:, None]
    strips = jnp.where(
        steps[None] >= 0, by_distance.T[:, np.maximum(np.minimum(steps, length - 1), 0)], masked_score
    )
    diagonals = pl.pallas_call(
        toeplitz_kernel,
        out_shape=jax.ShapeDtypeStruct((heads * tiles, 128, 128), F32),
        in_specs=[VMEM],
        out_specs=VMEM,
    )(strips.reshape(heads * tiles, 1, 256)).reshape(heads, tiles, 128, 128)
    blank = jnp.full((heads, 128, 128), masked_score)
    bias = jnp.concatenate(
        [
            jnp.concatenate([diagonals[:, i - j] if i >= j else blank for j in range(tiles)], 2)
            for i in range(tiles)
        ],
        1,
    )
    s1 = jnp.einsum("qhd,khd->hqk", q1, k1, preferred_element_type=F32) + bias
    p1 = jnp.exp(s1 - jnp.max(s1, -1, keepdims=True))
    p1 = p1 / jnp.sum(p1, -1, keepdims=True)
    p1_low = p1.astype(BF)
    o1 = jnp.einsum("hqk,khd->qhd", p1_low, v1, preferred_element_type=F32).astype(BF)
    o1 = o1.reshape(length, half)
    x1 = tokens + both(dot(o1, w_so, NT))
    h2 = rms_norm(x1, norm_gains[1]).astype(BF)
    q2 = dot(h2, c_q).astype(BF).reshape(length, heads, DH)
    total_blocks = tags.shape[0] // KB
    items = blocks * target_lengths.shape[0]
    most = total_blocks - items + 1
    owned = tags.reshape(total_blocks, KB)[:, 0] == rank
    order = jnp.argsort(jnp.logical_not(owned), stable=True)[:most]
    enc = encoder.reshape(total_blocks, KB, D)[order].reshape(most * KB, D)
    mine = (tags.reshape(total_blocks, KB)[order].reshape(most * KB) == rank)
    kc = dot(enc, c_k).astype(BF).reshape(-1, heads, DH)
    vc = dot(enc, c_v).astype(BF).reshape(-1, heads, DH)

    def cross_forward(parts):
        q, k, v = parts
        s = jnp.where(mine[None], dot(q, k, NT), masked_score)
        top = jnp.max(s, -1, keepdims=True)
        e = jnp.exp(s - top)
        total = jnp.sum(e, -1, keepdims=True)
        return (dot((e / total).astype(BF), v).astype(BF), top + jnp.log(total))

    by_head = lambda value: jnp.swapaxes(value.reshape(value.shape[0], heads, DH), 0, 1)
    q2h, kch, vch = by_head(q2), by_head(kc), by_head(vc)
    o2, lse = lax.map(cross_forward, (q2h, kch, vch))
    o2 = jnp.swapaxes(o2, 0, 1).reshape(length, half)
    x2 = x1 + both(dot(o2, w_co, NT))
    h3 = rms_norm(x2, norm_gains[2]).astype(BF)
    gate, upper = dot(h3, f_g), dot(h3, f_u)
    hidden_full, pull = jax.vjp(lambda g, u: jax.nn.gelu(g, approximate=True) * u, gate, upper)
    hidden = hidden_full.astype(BF)
    y = x2 + both(dot(hidden, f_d, NT))
    df = dy.astype(BF)
    g_fd = dot(df, hidden, TN)
    dgate, dup = (member.astype(BF) for member in pull(dot(df, f_d)))
    g_fg, g_fu = dot(h3, dgate, TN), dot(h3, dup, TN)
    dn3 = both(dot(dgate, f_g, NT) + dot(dup, f_u, NT))
    delta, gain3 = norm_back(x2, norm_gains[2], dn3)
    dx2 = dy + delta
    da2 = dx2.astype(BF)
    g_co = dot(da2, o2, TN)
    do2 = dot(da2, w_co).astype(BF)

    def cross_backward(parts):
        q, k, v, do, total = parts
        s = jnp.where(mine[None], dot(q, k, NT), masked_score)
        p = jnp.exp(s - total)
        dp = dot(do, v, NT)
        ds = (p * (dp - jnp.sum(p * dp, -1, keepdims=True))).astype(BF)
        return (
            dot(ds, k).astype(BF), dot(ds, q, TN).astype(BF), dot(p.astype(BF), do, TN).astype(BF)
        )

    dq2, dkc, dvc = lax.map(cross_backward, (q2h, kch, vch, by_head(do2), lse))
    flat_heads = lambda value: jnp.swapaxes(value, 0, 1).reshape(-1, half)
    dq2, dkc, dvc = flat_heads(dq2), flat_heads(dkc), flat_heads(dvc)
    g_cq, g_ck, g_cv = dot(h2, dq2, TN), dot(enc, dkc, TN), dot(enc, dvc, TN)
    enc_term = dot(dkc, c_k, NT) + dot(dvc, c_v, NT)
    spread = jnp.zeros((total_blocks, KB, D), BF).at[order].set(
        enc_term.astype(BF).reshape(most, KB, D)
    )
    encoder_grad = lax.psum_scatter(
        lax.psum_scatter(spread.reshape(-1, D), "mp", scatter_dimension=1, tiled=True),
        "blk", scatter_dimension=0, tiled=True,
    ).astype(F32)
    dn2 = both(dot(dq2, c_q, NT))
    delta, gain2 = norm_back(x1, norm_gains[1], dn2)
    dx1 = dx2 + delta
    da1 = dx1.astype(BF)
    g_so = dot(da1, o1, TN)
    do1 = dot(da1, w_so).astype(BF).reshape(length, heads, DH)
    dp1 = jnp.einsum("qhd,khd->hqk", do1, v1, preferred_element_type=F32)
    ds1 = (p1 * (dp1 - jnp.sum(p1 * dp1, -1, keepdims=True))).astype(BF)
    ds_wide = ds1.astype(F32)
    bucket_grid = jnp.asarray(bucket_of(np.maximum(spots[:, None] - spots[None, :], 0)).astype(np.int32))
    bias_sums = lax.map(
        lambda b: jnp.sum(jnp.where(bucket_grid[None] == b, ds_wide, 0.0), axis=(1, 2)),
        jnp.arange(position_bias.shape[0], dtype=jnp.int32),
    )
    grad_bias = lax.dynamic_update_slice_in_dim(
        jnp.zeros(position_bias.shape, F32), bias_sums, core * heads, 1
    )
    dq1 = jnp.einsum("hqk,khd->qhd", ds1, k1, preferred_element_type=F32)
    dk1 = jnp.einsum("hqk,qhd->khd", ds1, q1, preferred_element_type=F32)
    dv1 = jnp.einsum("hqk,qhd->khd", p1_low, do1, preferred_element_type=F32)
    dq1, dk1, dv1 = (member.astype(BF).reshape(length, half) for member in (dq1, dk1, dv1))
    g_q, g_k, g_v = dot(h1, dq1, TN), dot(h1, dk1, TN), dot(h1, dv1, TN)
    dn1 = both(dot(dq1, w_q, NT) + dot(dk1, w_k, NT) + dot(dv1, w_v, NT))
    delta, gain1 = norm_back(tokens, norm_gains[0], dn1)
    decoder_grad = dx1 + delta
    grads = jnp.concatenate(
        [member.astype(BF) for member in (g_q, g_k, g_v, g_so, g_cq, g_ck, g_cv, g_co, g_fg, g_fu, g_fd)],
        axis=1,
    )
    mine_grad = lax.psum_scatter(grads.astype(F32), "blk", scatter_dimension=0, tiled=True)
    pieces = [mine_grad[:, edges[index] : edges[index + 1]] for index in range(11)]
    shards = (
        jnp.stack(pieces[0:3]), pieces[3].T, jnp.stack(pieces[4:7]), pieces[7].T,
        jnp.stack(pieces[8:10]), pieces[10].T,
    )
    square_sum = jnp.sum(mine_grad * mine_grad)
    stat_terms = jnp.stack(
        [jnp.sum(valid * y * y), jnp.sum(valid * decoder_grad * decoder_grad), jnp.sum(valid)]
    )
    gain_grads, bias_grads, square_total, stat_total = lax.psum(
        (jnp.stack([gain1, gain2, gain3]) * 0.5, grad_bias, square_sum, stat_terms), ("blk", "mp")
    )
    grad_norm = jnp.sqrt(
        square_total + jnp.sum(gain_grads * gain_grads) + jnp.sum(bias_grads * bias_grads)
    )
    factor = jnp.minimum(1.0, clip_limit / (grad_norm + 1e-06))
    params = params + [norm_gains, position_bias]
    gradients = shards + (gain_grads, bias_grads)
    updated = [
        adamw(
            params[index], moments[index], moments[8 + index], gradients[index] * factor,
            weight_decay if index < 6 else 0.0, learn_rates[index],
        )
        for index in range(8)
    ]
    token_rms = jnp.sqrt(stat_total[:2] / (stat_total[2] * D))
    own = lambda value: lax.dynamic_slice_in_dim(value, core * rows_own, rows_own, 0)
    return (
        own(y).astype(BF),
        own(decoder_grad),
        encoder_grad,
        *(entry[0] for entry in updated),
        *(entry[1] for entry in updated),
        *(entry[2] for entry in updated),
        grad_norm,
        token_rms,
    )


def solution(mesh):
    proj, out = P(None, "blk", "mp"), P("mp", "blk")
    family = (proj, out, proj, out, proj, out, P(), P())
    tokens = P(("blk", "mp"), None)
    tiled = mesh.shape["blk"] == 16 and D // mesh.shape["blk"] % 16 == 0
    return jax.shard_map(
        fused if tiled else plain_body,
        mesh=mesh,
        in_specs=(tokens, P("blk", None), tokens, P("blk"), P("blk"), P("blk")) + family * 3,
        out_specs=(tokens, tokens, P("blk", "mp")) + family * 3 + (P(), P()),
        check_vma=False,
    )
```

```python
import functools
import math

import jax
import jax.numpy as jnp
import numpy as np
from jax import lax
from jax.experimental import pallas as pl
from jax.experimental.pallas import tpu as pltpu
from jax.sharding import PartitionSpec as P

D = 768
DH = 64
KB = 64
STEP = 10
MESH = pl.DeviceIdType.MESH
ANY = pl.BlockSpec(memory_space=pl.ANY)
VMEM = pl.BlockSpec(memory_space=pltpu.VMEM)

norm_eps = 1e-06
clip_limit = 1.0
learn_rates = (0.02, 0.2, 0.02, 0.5, 0.02, 0.02, 1.0, 0.5)
beta_one = 0.9
beta_two = 0.999
adam_eps = 1e-08
weight_decay = 0.01
masked_score = -1000000000.0
HIGHEST = lax.Precision.HIGHEST
BF = jnp.bfloat16
F32 = jnp.float32
edge_table = np.ceil(16.0 * 8.0 ** (np.arange(16) / 16.0)).astype(np.int32)


def bucket_of(distance):
    above = np.sum(distance[..., None] >= edge_table, axis=-1)
    return np.where(distance < 16, distance, 15 + above)


def rms_norm(values, gain):
    return values * lax.rsqrt(jnp.mean(values * values, axis=-1, keepdims=True) + norm_eps) * gain


def norm_back(values, gain, upstream):
    scale = lax.rsqrt(jnp.mean(values * values, axis=-1, keepdims=True) + norm_eps)
    weighted = upstream * gain
    inner = jnp.mean(weighted * values, axis=-1, keepdims=True)
    return (
        scale * weighted - values * scale * scale * scale * inner,
        jnp.sum(upstream * values * scale, axis=0),
    )


def adamw(weight, moment, second, grad, decay, rate):
    moment = beta_one * moment + (1.0 - beta_one) * grad
    second = beta_two * second + (1.0 - beta_two) * grad * grad
    fixed_first = moment / (1.0 - beta_one**STEP)
    fixed_second = second / (1.0 - beta_two**STEP)
    weight = weight - rate * (fixed_first / (jnp.sqrt(fixed_second) + adam_eps) + decay * weight)
    return (weight, moment, second)


def toeplitz_kernel(strip_ref, out_ref):
    @pl.loop(0, strip_ref.shape[0])
    def _(index):
        rows = jnp.broadcast_to(strip_ref[index], (128, 256))
        out_ref[index] = pltpu.roll(rows, 0, 1, stride=1, stride_axis=0)[:, :128]


class Place:
    def __init__(self, levels):
        self.levels = levels
        self.long = 2**levels
        self.me = lax.axis_index("blk")
        self.core = lax.axis_index("mp")
        self.p = lax.rem(self.me, 4)
        self.a = self.me // 4
        x = lax.rem(self.p, 2)
        y = self.p // 2
        dx = 1 - 2 * x
        dy = 2 - 4 * y
        d_first = dx + self.core * (dy - dx)
        d_second = dy + self.core * (dx - dy)
        self.p_first = self.p + d_first
        self.p_second = self.p + d_second
        self.p_both = self.p + dx + dy
        self.first = {"blk": self.me + d_first}
        self.second = {"blk": self.me + d_second}
        self.sibling = {"mp": 1 - self.core}
        self.in_plane = 2 * self.p + self.core

    def group(self, level):
        return (self.a // 2**level) * 2**level

    def other_group(self, level):
        bit = lax.rem(self.a // 2**level, 2)
        return self.group(level) + (1 - 2 * bit) * 2**level

    def partner(self, level):
        bit = lax.rem(self.a // 2**level, 2)
        return {"blk": self.me + (1 - 2 * bit) * 2**level * 4}

    def partners(self):
        near = [self.partner(level) for level in range(self.levels)]
        return near + [self.first, self.second, self.sibling]

    def plane_mate(self, step):
        other = lax.rem(self.in_plane + step, 8)
        return {"blk": self.me - self.p + other // 2, "mp": lax.rem(other, 2)}

    def line_mate(self, step):
        return {"blk": self.me + 4 * (lax.rem(self.a + step, self.long) - self.a)}

    def mates(self):
        return [self.plane_mate(step) for step in range(1, 8)] + [
            self.line_mate(step) for step in range(1, self.long)
        ]


def enter(partners):
    barrier = pltpu.get_barrier_semaphore()
    for device in partners:
        pl.semaphore_signal(barrier, inc=1, device_id=device, device_id_type=MESH)
    pl.semaphore_wait(barrier, len(partners))


class Copies:
    def __init__(self, send, recv):
        self.send, self.recv, self.count, self.open = send, recv, 0, []

    def remote(self, src, dst, device):
        index = self.count
        self.count += 1
        copy = pltpu.make_async_remote_copy(
            src_ref=src,
            dst_ref=dst,
            send_sem=self.send.at[index],
            recv_sem=self.recv.at[index],
            device_id=device,
            device_id_type=MESH,
        )
        copy.start()
        self.open.append(copy)
        return copy

    def left(self, copy):
        copy.wait_send()
        self.open = [member for member in self.open if member is not copy]

    def finish(self):
        for copy in self.open:
            copy.wait_send()
        self.open = []


class Moves:
    def __init__(self, semaphores):
        self.semaphores, self.count, self.open = semaphores, 0, {}

    def start(self, name, src, dst):
        copy = pltpu.make_async_copy(src, dst, self.semaphores.at[self.count])
        self.count += 1
        copy.start()
        self.open[name] = copy

    def need(self, *names):
        for name in names:
            if name in self.open:
                self.open.pop(name).wait()

    def finish(self):
        self.need(*list(self.open))


def dot(left, right, dims=((1,), (0,))):
    return lax.dot_general(left, right, (dims, ((), ())), preferred_element_type=F32)


NN = ((1,), (0,))
NT = ((1,), (1,))


LINK_BYTES = 1e5
DELAY = 1.5


class Pump:
    def __init__(self, gate, ahead, backlog, pace):
        self.now = 0.0
        self.free = {}
        self.flying = []
        self.count = 0
        self.pending = []
        self.gate, self.ahead, self.backlog, self.pace = gate, ahead, backlog, pace

    def _resume(self, chain):
        try:
            loads, after = next(chain)
        except StopIteration:
            return
        for link, size in loads.items():
            self.free[link] = max(self.free.get(link, 0.0), self.now) + size / LINK_BYTES
        self.count += 1
        end = max(self.free[link] for link in loads)
        self.flying.append((end + DELAY, self.count, chain, after))

    def _ready(self, entry):
        return max(entry[0], self.free.get(entry[3], 0.0) - self.backlog)

    def _start(self):
        while self.pending and self.free.get(self.gate, 0.0) <= self.now + self.ahead:
            self._resume(self.pending.pop(0))

    def _next(self):
        soonest = min(self.flying, key=lambda entry: (self._ready(entry), entry[1]))
        self.flying = [entry for entry in self.flying if entry is not soonest]
        self.now = max(self.now, self._ready(soonest))
        self._resume(soonest[2])
        self._start()

    def add(self, *chains):
        self.pending.extend(chains)
        self._start()

    def work(self, spent):
        end = self.now + self.pace * spent
        while self.flying and min(self._ready(entry) for entry in self.flying) <= end:
            self._next()
        self.now = max(self.now, end)
        self._start()

    def until(self, chain):
        busy = lambda: any(entry[2] is chain for entry in self.flying)
        while busy() or any(member is chain for member in self.pending):
            if not self.flying:
                self.now = max(self.now, self.free.get(self.gate, 0.0) - self.ahead)
                self._start()
            else:
                self._next()

    def drain(self):
        while self.flying or self.pending:
            if not self.flying:
                self.now = max(self.now, self.free.get(self.gate, 0.0) - self.ahead)
                self._start()
            else:
                self._next()


def bytes_of(ref):
    size = 2 if ref.dtype == BF else 4
    return size * int(np.prod(ref.shape))


EVERY = slice(None)


class View:
    def __init__(self, ref, *lead, columns=slice(None)):
        self.ref, self.lead, self.columns = ref, lead, columns

    def _index(self, index):
        index = self.lead + index
        return index + (EVERY,) * (len(self.ref.shape) - 1 - len(index)) + (self.columns,)

    def at(self, *index):
        return self.ref.at[self._index(index)]

    def get(self, *index):
        return self.ref[self._index(index)]

    def put(self, value, *index):
        self.ref[self._index(index)] = value.astype(self.ref.dtype)


def line_load(level, size):
    return {"ends": size} if level == 0 else {"ends": 2**level * size, "middle": 4**level * size}


def gather_chain(place, copies, slot, plane_first=False):
    unit = 2.0 * bytes_of(slot(0, 0))

    def plane(a, weight, after):
        one = copies.remote(slot(a, place.p), slot(a, place.p), place.first)
        two = copies.remote(slot(a, place.p), slot(a, place.p), place.second)
        yield {"xy": unit * weight}, "xy"
        two.wait_recv()
        three = copies.remote(slot(a, place.p_second), slot(a, place.p_second), place.first)
        yield {"xy": unit * weight / 2}, after
        one.wait_recv()
        three.wait_recv()

    def line(p, weight, after):
        for level in range(place.levels):
            zs = place.a if level == 0 else pl.ds(place.group(level), 2**level)
            sent = copies.remote(slot(zs, p), slot(zs, p), place.partner(level))
            yield line_load(level, unit * weight), "middle" if level + 1 < place.levels else after
            sent.wait_recv()

    if plane_first:
        yield from plane(place.a, 1, "ends")
        yield from line(EVERY, 4, None)
    else:
        yield from line(place.p, 1, "xy")
        yield from plane(EVERY, place.long, None)


def add_up(*terms):
    if len(terms) == 2 and terms[0].dtype == terms[1].dtype:
        return terms[0] + terms[1]
    total = terms[0].astype(F32)
    for term in terms[1:]:
        total = total + term.astype(F32)
    return total


def scatter_chain(place, copies, grads, two, one, total, zs, out):
    long = place.long
    unit = 2.0 * bytes_of(grads.at(0, 0))
    far = copies.remote(grads.at(EVERY, place.p_both), two.at(1), place.first)
    near = copies.remote(grads.at(EVERY, place.p_first), two.at(0), place.first)
    yield {"xy": unit * long}, "xy"
    far.wait_recv()

    for z in range(long):
        total.put(add_up(grads.get(z, place.p_second), two.get(1, z)), z)

    last = copies.remote(total.at(), one.at(), place.second)
    yield {"xy": unit * long / 2}, "middle"
    near.wait_recv()
    last.wait_recv()
    copies.left(last)
    sent = []

    for z in range(long):
        total.put(add_up(grads.get(z, place.p), two.get(0, z), one.get(z)), z)

    for level in reversed(range(place.levels)):
        away = pl.ds(place.other_group(level), 2**level)
        landing = pl.ds(2**level - 1, 2**level)
        copy = copies.remote(total.at(away), zs.at(landing), place.partner(level))
        sent.append(copy)
        yield line_load(level, unit), "ends" if level > 0 else None
        copy.wait_recv()
        if level == 0:
            out.put(total.get(place.a).astype(F32) + zs.get(0).astype(F32))
        else:
            for z in range(2**level):
                mine = place.group(level) + z
                total.put(add_up(total.get(mine), zs.get(2**level - 1 + z)), mine)
    for copy in sent:
        copies.left(copy)


def scatter_line_first(place, copies, grads, two, one, total, zs, out):
    unit = 2.0 * bytes_of(grads.at(0, 0))
    top = place.levels - 1
    local = lambda z: lax.rem(z, 2**top)
    for level in reversed(range(place.levels)):
        source, at = (grads, lambda z: z) if level == top else (total, local)
        away = pl.ds(at(place.other_group(level)), 2**level)
        landing = pl.ds(2**level - 1, 2**level)
        copy = copies.remote(source.at(away), zs.at(landing), place.partner(level))
        yield line_load(level, 4 * unit), "ends" if level > 0 else "xy"
        copy.wait_recv()

        for z in range(2**level):
            mine = place.group(level) + z
            for p in range(4):
                total.put(
                    add_up(source.get(at(mine), p), zs.get(2**level - 1 + z, p)), local(mine), p
                )

    here = local(place.a)
    far = copies.remote(total.at(here, place.p_both), two.at(1), place.first)
    near = copies.remote(total.at(here, place.p_first), two.at(0), place.first)
    yield {"xy": unit}, "xy"
    far.wait_recv()
    total.put(add_up(total.get(here, place.p_second), two.get(1)), here, place.p_second)
    last = copies.remote(total.at(here, place.p_second), one.at(), place.second)
    yield {"xy": unit / 2}, None
    near.wait_recv()
    last.wait_recv()
    out.put(add_up(total.get(here, place.p), two.get(0), one.get()))


def sum_chain(place, copies, mine, plane, middle, line, out):
    plane[place.in_plane] = mine[...]
    sent = [
        copies.remote(mine, plane.at[place.in_plane], place.plane_mate(step)) for step in range(1, 8)
    ]
    yield {"xy": 0.0}, "middle"
    for copy in sent:
        copy.wait_recv()
    total = plane[0]
    for index in range(1, 8):
        total = total + plane[index]
    middle[...] = total
    line[place.a] = total
    sent = [
        copies.remote(middle, line.at[place.a], place.line_mate(step))
        for step in range(1, place.long)
    ]
    yield {"middle": 0.0}, None
    for copy in sent:
        copy.wait_recv()
    total = line[0]
    for index in range(1, place.long):
        total = total + line[index]
    out[...] = total


def norm_rows(values, gain):
    return values * lax.rsqrt(jnp.mean(values * values, axis=-1, keepdims=True) + norm_eps) * gain


def head_mask(which):
    lane = lax.broadcasted_iota(jnp.int32, (1, 128), 1)
    return jnp.where(lane // DH == which, 1.0, 0.0).astype(BF)


def make_eye(eye):
    row = lax.broadcasted_iota(jnp.int32, eye.shape, 0)
    column = lax.broadcasted_iota(jnp.int32, eye.shape, 1)
    eye[...] = jnp.where(row == column, 1.0, 0.0).astype(BF)


def turn(value, eye):
    parts = []
    for start in range(0, value.shape[1], 256):
        size = min(256, value.shape[1] - start)
        piece = value[:, start : start + size]
        parts.append(dot(eye[pl.ds(0, size), pl.ds(0, size)], piece, NT).astype(BF))
    return parts[0] if len(parts) == 1 else jnp.concatenate(parts, axis=0)


def lanes_at(start, pair):
    return pl.ds(start + pair * 128, 128)


CHUNK = 64


def bias_rows(bias, head, tiles, tile, key):
    blank = jnp.full((128, 128), masked_score, F32)
    away = [2 * tile - key, 2 * tile + 1 - key]
    return jnp.concatenate(
        [bias[head * tiles + each] if each >= 0 else blank for each in away], axis=1
    )


def grouped(chunk):
    return chunk.reshape(chunk.shape[0] // 8, 8, chunk.shape[1])


def eight_rows(row):
    return jnp.broadcast_to(row, (8, row.shape[1]))[None]


def softmax_chunks(load, chunks, low_out):
    top = None
    for index in range(chunks):
        most = jnp.max(grouped(load(index)), axis=0)
        top = most if top is None else jnp.maximum(top, most)
    top = jnp.max(top, axis=0, keepdims=True)
    wide_top = eight_rows(top)
    total = None
    for index in range(chunks):
        shifted = jnp.exp(grouped(load(index)) - wide_top)
        part = jnp.sum(shifted, axis=0)
        total = part if total is None else total + part
        low_out(index, shifted.reshape(CHUNK, shifted.shape[2]).astype(BF))
    total = jnp.sum(total, axis=0, keepdims=True)
    return (total, top + jnp.log(total))


def back_chunk(scores, dprobs, log_total, inner):
    probs = jnp.exp(grouped(scores) - log_total)
    dscores = probs * (grouped(dprobs) - inner)
    return (probs.reshape(scores.shape).astype(BF), dscores.reshape(scores.shape).astype(BF))


def self_forward(pair, qkv, bias, o1, o1_turned, lse, eye, scores, low_probs, between):
    width = o1.shape[1]
    tiles = qkv.shape[0] // 128
    values_turned = turn(qkv[:, lanes_at(2 * width, pair)], eye)
    for tile in range(tiles // 2):
        rows, seen = pl.ds(tile * 256, 256), (tile + 1) * 256
        query = qkv[rows, lanes_at(0, pair)]
        key = qkv[pl.ds(0, seen), lanes_at(width, pair)]
        made = []
        for which in range(2):
            head = 2 * pair + which
            scores[which, pl.ds(0, seen), :] = dot(key, query * head_mask(which), NT)

            def load(index):
                block = bias_rows(bias, head, tiles, tile, index // 2)
                at = (index % 2) * CHUNK
                return scores[which, pl.ds(index * CHUNK, CHUNK), :] + block[at : at + CHUNK]

            def low_out(index, value):
                low_probs[which, pl.ds(index * CHUNK, CHUNK), :] = value

            total, log_total = softmax_chunks(load, seen // CHUNK, low_out)
            lse[pl.ds(head, 1), rows] = log_total
            value = values_turned[which * DH : (which + 1) * DH, :seen]
            made.append(dot(value, low_probs[which, pl.ds(0, seen), :]) * (1.0 / total))
        made = jnp.concatenate(made, axis=0)
        o1_turned[lanes_at(0, pair), rows] = made
        o1[rows, lanes_at(0, pair)] = turn(made.astype(BF), eye)
        between()


def inner_rows(pair, which, o_turned, do_turned):
    here = pl.ds(pair * 128 + which * DH, DH)
    upstream = do_turned[which * DH : (which + 1) * DH, :].astype(F32)
    return eight_rows(jnp.sum(o_turned[here, :] * upstream, axis=0, keepdims=True))


def self_backward(
    pair, qkv, bias, lse, o1_turned, do1, dqkv, buckets, bias_total, eye,
    scores, dprobs, low_probs, low_dscores, between,
):
    width = do1.shape[1]
    length = qkv.shape[0]
    tiles = length // 128
    keys_turned = turn(qkv[:, lanes_at(width, pair)], eye)
    do_turned = turn(do1[:, lanes_at(0, pair)], eye)
    queries, upstreams = [], []
    for tile in range(tiles // 2):
        rows, seen = pl.ds(tile * 256, 256), (tile + 1) * 256
        query = qkv[rows, lanes_at(0, pair)]
        key = qkv[pl.ds(0, seen), lanes_at(width, pair)]
        value = qkv[pl.ds(0, seen), lanes_at(2 * width, pair)]
        upstream = do1[rows, lanes_at(0, pair)]
        made = []
        for which in range(2):
            head = 2 * pair + which
            at = pl.ds((2 * tile + which) * 256, 256)
            queries.append(query * head_mask(which))
            upstreams.append(upstream * head_mask(which))
            inner = inner_rows(pair, which, o1_turned.at[:, rows], do_turned[:, tile * 256 : seen])
            scores[which, pl.ds(0, seen), :] = dot(key, queries[-1], NT)
            dprobs[which, pl.ds(0, seen), :] = dot(value, upstreams[-1], NT)
            log_total = eight_rows(lse[pl.ds(head, 1), rows])
            for index in range(seen // CHUNK):
                here = pl.ds(index * CHUNK, CHUNK)
                block = bias_rows(bias, head, tiles, tile, index // 2)
                start = (index % 2) * CHUNK
                value_here = scores[which, here, :] + block[start : start + CHUNK]
                low_probs[here, at], low_dscores[here, at] = back_chunk(
                    value_here, dprobs[which, here, :], log_total, inner
                )
            made.append(
                dot(keys_turned[which * DH : (which + 1) * DH, :seen], low_dscores[pl.ds(0, seen), at])
            )
        dqkv[rows, lanes_at(0, pair)] = turn(jnp.concatenate(made, axis=0).astype(BF), eye)
        between()
    queries = jnp.concatenate(queries, axis=0)
    upstreams = jnp.concatenate(upstreams, axis=0)
    for tile in range(tiles // 2):
        rows, later = pl.ds(tile * 256, 256), pl.ds(tile * 512, 2 * length - tile * 512)
        dkey = dot(low_dscores[rows, later], queries[tile * 512 :])
        dqkv[rows, lanes_at(width, pair)] = dkey.astype(BF)
        dvalue = dot(low_probs[rows, later], upstreams[tile * 512 :])
        dqkv[rows, lanes_at(2 * width, pair)] = dvalue.astype(BF)
    for which in range(2):
        total = jnp.zeros((8, 128), F32)
        for away in range(tiles):
            summed = None
            for key in range(tiles - away):
                query = key + away
                start = (2 * (query // 2) + which) * 256 + (query % 2) * 128
                block = low_dscores[pl.ds(key * 128, 128), pl.ds(start, 128)].astype(F32)
                summed = block if summed is None else summed + block
            total = total + lax.dot_general(
                diagonal_sums(summed), buckets[away].astype(F32), (NN, ((), ())), precision=HIGHEST,
                preferred_element_type=F32,
            )
        row = lax.broadcasted_iota(jnp.int32, (8, 128), 0)
        bias_total[...] += jnp.where(row == 2 * pair + which, total, 0.0)


def diagonal_sums(tile):
    wide = jnp.concatenate([tile, jnp.zeros_like(tile)], axis=1)
    turned = wide[0:8]
    for group in range(1, 16):
        turned = turned + pltpu.roll(wide[8 * group : 8 * group + 8], 256 - 8 * group, 1)
    place_in = lax.broadcasted_iota(jnp.int32, (8, 256), 0)
    for bit in (1, 2, 4):
        moved = pltpu.roll(turned, 256 - bit, 1)
        turned = jnp.where(lax.rem(place_in // bit, 2) == 1, moved, turned)
    return jnp.broadcast_to(jnp.sum(turned, axis=0, keepdims=True), (8, 256))


def lane_row(index):
    lane = lax.broadcasted_iota(jnp.int32, (1, 128), 1)
    return jnp.where(lane == index, 1.0, 0.0).astype(BF)


def with_mask(key, mask, which):
    spot = lane_row((1 - which) * DH)
    return key * (1 - spot) + mask * spot


def with_one(query, which):
    return query * head_mask(which) + lane_row((1 - which) * DH)


def cross_forward(pair, q2, kc, vc, mask, o2, o2_turned, lse, eye, scores, low_probs, between):
    values_turned = turn(vc[:, lanes_at(0, pair)], eye)
    key = kc[:, lanes_at(0, pair)]
    keys = [with_mask(key, mask[...], which) for which in range(2)]
    for tile in range(q2.shape[0] // 256):
        rows = pl.ds(tile * 256, 256)
        query = q2[rows, lanes_at(0, pair)]
        made = []
        for which in range(2):
            scores[which] = dot(keys[which], with_one(query, which), NT)

            def load(index):
                return scores[which, pl.ds(index * CHUNK, CHUNK), :]

            def low_out(index, value):
                low_probs[which, pl.ds(index * CHUNK, CHUNK), :] = value

            total, log_total = softmax_chunks(load, key.shape[0] // CHUNK, low_out)
            lse[pl.ds(2 * pair + which, 1), rows] = log_total
            value = values_turned[which * DH : (which + 1) * DH, :]
            made.append(dot(value, low_probs[which]) * (1.0 / total))
        made = jnp.concatenate(made, axis=0)
        o2_turned[lanes_at(0, pair), rows] = made
        o2[rows, lanes_at(0, pair)] = turn(made.astype(BF), eye)
        between()


def cross_backward(
    pair, q2, kc, vc, mask, lse, o2_turned, do2, dq2, dkc, dvc, eye,
    scores, dprobs, low_probs, low_dscores, between,
):
    key, value = kc[:, lanes_at(0, pair)], vc[:, lanes_at(0, pair)]
    keys = [with_mask(key, mask[...], which) for which in range(2)]
    keys_turned = turn(key, eye)
    do_turned = turn(do2[:, lanes_at(0, pair)], eye)
    queries, upstreams = [], []
    for tile in range(q2.shape[0] // 256):
        rows = pl.ds(tile * 256, 256)
        query, upstream = q2[rows, lanes_at(0, pair)], do2[rows, lanes_at(0, pair)]
        made = []
        for which in range(2):
            at = pl.ds((2 * tile + which) * 256, 256)
            queries.append(query * head_mask(which))
            upstreams.append(upstream * head_mask(which))
            inner = inner_rows(
                pair, which, o2_turned.at[:, rows], do_turned[:, tile * 256 : (tile + 1) * 256]
            )
            scores[which] = dot(keys[which], with_one(query, which), NT)
            dprobs[which] = dot(value, upstreams[-1], NT)
            log_total = eight_rows(lse[pl.ds(2 * pair + which, 1), rows])
            for index in range(key.shape[0] // CHUNK):
                here = pl.ds(index * CHUNK, CHUNK)
                low_probs[here, at], low_dscores[here, at] = back_chunk(
                    scores[which, here, :], dprobs[which, here, :], log_total, inner
                )
            made.append(dot(keys_turned[which * DH : (which + 1) * DH, :], low_dscores[:, at]))
        dq2[rows, lanes_at(0, pair)] = turn(jnp.concatenate(made, axis=0).astype(BF), eye)
        between()
    dkc[:, lanes_at(0, pair)] = dot(low_dscores[...], jnp.concatenate(queries, axis=0)).astype(BF)
    dvc[:, lanes_at(0, pair)] = dot(low_probs[...], jnp.concatenate(upstreams, axis=0)).astype(BF)


def row_tiles(length):
    def run(step):
        for tile in range(length // 64):
            step(tile)

    return run


def rows_of(tile):
    return pl.ds(tile * 64, 64)


def back_through_norm(values, gain, upstream):
    scale = lax.rsqrt(jnp.mean(values * values, axis=-1, keepdims=True) + norm_eps)
    weighted = upstream * gain
    inner = jnp.mean(weighted * values, axis=-1, keepdims=True)
    return (
        scale * weighted - values * (scale * scale * scale * inner),
        jnp.sum(upstream * values * scale, axis=0, keepdims=True),
    )


def feed_tile(
    tile, h3, df, h3_turned, df_turned, feed, y_part, dn_part, g_feed, width,
    gate_up, dhidden, hidden, dpair,
):
    up_down = columns_of(feed, tile, 0, 2 * width)
    down = columns_of(feed, tile, 2 * width, width)
    gate_up[...] = dot(h3[...], up_down)
    dhidden[...] = dot(df[...], down)
    root = math.sqrt(2.0 / math.pi)

    @row_tiles(h3.shape[0])
    def _(index):
        rows = rows_of(index)
        gate, upper = gate_up[rows, pl.ds(0, width)], gate_up[rows, pl.ds(width, width)]
        upstream = dhidden[rows, :]
        square = gate * gate
        curve = jnp.tanh(gate * (root + root * 0.044715 * square))
        half = 0.5 + 0.5 * curve
        active = gate * half
        slope = half + 0.5 * gate * (1.0 - curve * curve) * (root + root * 3 * 0.044715 * square)
        hidden[rows, :] = (active * upper).astype(BF)
        dpair[rows, pl.ds(0, width)] = (upstream * upper * slope).astype(BF)
        dpair[rows, pl.ds(width, width)] = (upstream * active).astype(BF)

    y_now = dot(hidden[...], down, NT)
    dn_now = dot(dpair[...], up_down, NT)
    if tile == 0:
        y_part[...] = y_now
        dn_part[...] = dn_now
    else:
        y_part[...] += y_now
        dn_part[...] += dn_now
    put_columns(g_feed, tile, 0, dot(h3_turned[...], dpair[...]))
    put_columns(g_feed, tile, 2 * width, dot(df_turned[...], hidden[...]))


FEED_TILE = 256
PIECE = 768


def columns_of(ref, piece, start, count):
    value = ref[piece, :, :, :, pl.ds(start, count)]
    return value.reshape(value.shape[0] * value.shape[1] * value.shape[2], count)


def put_columns(ref, piece, start, value):
    ref[piece, :, :, :, pl.ds(start, value.shape[1])] = value.astype(ref.dtype).reshape(
        ref.shape[1:4] + (value.shape[1],)
    )


def swap_rows(copies, place, part, got, left, weights):
    sent = []
    for start in range(0, part.shape[0], 256):
        rows = pl.ds(start, 256)
        total, first = None, 0
        for weight in weights:
            columns = pl.ds(first, weight.shape[1])
            first += weight.shape[1]
            value = dot(left[rows, columns], weight, NT)
            total = value if total is None else total + value
        part[rows, :] = total.astype(part.dtype)
        sent.append(copies.remote(part.at[rows, :], got.at[rows, :], place.sibling))
    return sent


def both_parts(part, got, rows):
    return part[rows, :].astype(F32) + got[rows, :].astype(F32)


def arrived(sent, tile):
    if tile % 4 == 0:
        sent[tile // 4].wait_recv()


FRONT_OUT = (
    "near", "bias", "h1_turned", "qkv", "lse1", "o1", "o1_turned", "x1", "h2_turned", "q2", "enc_mine", "kc", "vc",
    "mask", "lse2", "o2", "o2_turned", "dx2", "g_feed", "layer_out", "stats",
)


def front_kernel(
    levels, slots,
    self_proj, self_out, cross_proj, cross_out, feed_in, feed_out, encoder, tok_own, grad_own,
    gains, bias_table, one_hot, blank, items, lengths, limit, *refs,
):
    outs = dict(zip(FRONT_OUT, refs))
    slot_of = refs[len(FRONT_OUT)]
    refs = refs[len(FRONT_OUT) + 1 :]
    kept = dict(zip(FRONT_OUT, refs))
    (
        near, bias, h1_turned, qkv, lse1, o1, o1_turned, x1, h2_turned, q2, enc_mine, kc, vc, mask,
        lse2, o2, o2_turned, dx2, g_feed, layer_out, stats,
    ) = refs[: len(FRONT_OUT)]
    (
        scores, low_probs, gate_up, dhidden, hidden, dpair, feed, enc, info, scalars, tok, grad,
        part_one, part_two, y_part, dn_part, y_low, dn_low, got_one, got_two, got_y, got_dn, x2, h3, df,
        h3_turned,
        df_turned, eye, strips, h1, h2, send, recv, local,
    ) = refs[len(FRONT_OUT) :]
    place = Place(levels)
    enter(place.partners())
    copies, moves = Copies(send, recv), Moves(local)
    length, width = o1.shape
    half_rows = length // 2
    keep = lambda *names: [moves.start(name, kept[name], outs[name]) for name in names]
    tok_sent = copies.remote(tok_own, tok.at[place.core], place.sibling)

    def pack(piece, start, value):
        target = near if piece < near.shape[0] else feed
        at = pl.ds(start, value.shape[1])
        target[piece % near.shape[0], place.a, place.p, :, at] = value.astype(BF)

    def pack_projections(base, proj, out):
        pack(base, 0, proj[0])
        pack(base, width, proj[1])
        pack(base + 1, 0, proj[2])
        pack(base + 1, width, out[...])

    row = lax.broadcasted_iota(jnp.int32, (8, 128), 0)
    lane = lax.broadcasted_iota(jnp.int32, (8, 128), 1)
    known = jnp.zeros((8, 128), jnp.int32)
    per_chip = enc.shape[3]
    for index in range(per_chip):
        pair = jnp.where(lane == 0, items[index], jnp.where(lane == 1, lengths[index], 0))
        known = jnp.where(row == index, pair, known)
    info[place.a, place.p] = known
    pack_projections(0, self_proj, self_out)
    pump = Pump("ends", 1.5, 2.0, 1.0)

    def piece(index):
        target = near if index < near.shape[0] else feed
        return gather_chain(
            place, copies, lambda a, p: target.at[index % near.shape[0], a, p],
            plane_first=index in (3, 7),
        )

    pieces = [piece(index) for index in range(near.shape[0] + feed.shape[0])]
    info_chain = gather_chain(place, copies, lambda a, p: info.at[a, p])
    enc_chain = gather_chain(place, copies, lambda a, p: enc.at[place.core, a, p])
    pump.add(info_chain, pieces[0], pieces[1])
    half_cols = enc.shape[5]
    own_cols = pl.ds(pl.multiple_of(place.core * half_cols, half_cols), half_cols)
    enc[place.core, place.a, place.p] = encoder[:, own_cols].reshape(per_chip, KB, half_cols)
    pack_projections(2, cross_proj, cross_out)
    for tile in range(feed.shape[0]):
        at = pl.ds(tile * FEED_TILE, FEED_TILE)
        pack(4 + tile, 0, feed_in[0, :, at])
        pack(4 + tile, FEED_TILE, feed_in[1, :, at])
        pack(4 + tile, 2 * FEED_TILE, feed_out[:, at])
    pump.add(enc_chain, pieces[3], pieces[2], *pieces[4:])
    grad_sent = copies.remote(grad_own, grad.at[place.core], place.sibling)
    tok[place.core] = tok_own[...]
    grad[place.core] = grad_own[...]
    lse1[...] = jnp.zeros_like(lse1)
    lse2[...] = jnp.zeros_like(lse2)
    make_eye(eye)
    heads = width // DH
    strips[pl.ds(0, bias_table.shape[0]), :] = blank[...] + lax.dot_general(
        bias_table[...], one_hot[...], (NN, ((), ())), precision=HIGHEST, preferred_element_type=F32
    )
    tiles = length // 128
    for head in range(heads):
        for tile in range(tiles):
            strip = strips[pl.ds(place.core * heads + head, 1), pl.ds(tile * 256, 256)]
            rows = jnp.broadcast_to(strip, (128, 256))
            bias[head * tiles + tile] = pltpu.roll(rows, 0, 1, stride=1, stride_axis=0)[:, :128]
    keep("bias")
    pump.work(3.0)
    tok_sent.wait_recv()

    @row_tiles(length)
    def _(tile):
        part = tile // (half_rows // 64)
        values = tok[part, rows_of(tile - part * (half_rows // 64)), :].astype(F32)
        h1[rows_of(tile), :] = norm_rows(values, gains[0:1, :]).astype(BF)

    h1_turned[...] = turn(h1[...], eye)
    keep("h1_turned")
    grad_sent.wait_recv()
    top = limit[0]

    @row_tiles(length)
    def _(tile):
        part = tile // (half_rows // 64)
        rows = rows_of(tile)
        row = lax.broadcasted_iota(jnp.int32, (64, 1), 0) + tile * 64
        values = grad[part, rows_of(tile - part * (half_rows // 64)), :].astype(F32)
        df[rows, :] = jnp.where(row < top, values, 0.0).astype(BF)

    df_turned[...] = turn(df[...], eye)
    pump.work(2.0)
    pump.until(pieces[0])
    qkv[:, pl.ds(0, 2 * width)] = dot(h1[...], columns_of(near, 0, 0, 2 * width)).astype(BF)
    pump.work(2.0)
    pump.until(pieces[1])
    qkv[:, pl.ds(2 * width, width)] = dot(h1[...], columns_of(near, 1, 0, width)).astype(BF)
    keep("qkv")
    pump.work(1.0)
    for pair in range(width // 128):
        self_forward(
            pair, qkv, bias, o1, o1_turned, lse1, eye, scores, low_probs, lambda: pump.work(1.5)
        )
    keep("lse1", "o1", "o1_turned")
    one_sent = swap_rows(copies, place, part_one, got_one, o1, [columns_of(near, 1, width, width)])
    pump.work(1.0)
    pump.until(enc_chain)
    enc_sent = copies.remote(enc.at[place.core], enc.at[place.core], place.sibling)
    pump.until(info_chain)
    moves.start("info", info, scalars)
    pump.work(2.0)

    @row_tiles(length)
    def _(tile):
        arrived(one_sent, tile)
        rows = rows_of(tile)
        part = tile // (half_rows // 64)
        values = tok[part, rows_of(tile - part * (half_rows // 64)), :].astype(F32)
        values = values + both_parts(part_one, got_one, rows)
        x1[rows, :] = values
        h2[rows, :] = norm_rows(values, gains[1:2, :]).astype(BF)

    keep("x1")
    h2_turned[...] = turn(h2[...], eye)
    keep("h2_turned")
    moves.need("info")
    total_blocks = enc.shape[1] * 4 * per_chip

    def block_at(block):
        chip = block // per_chip
        return (chip // 4, lax.rem(chip, 4), lax.rem(block, per_chip))

    def look(block, carried):
        count, found, sizes = carried
        z, p, at = block_at(block)
        own = (scalars[z, p, at, 0] == place.me).astype(jnp.int32)
        slot_of[block] = own * count + (1 - own) * slots
        here = [own * (count == index).astype(jnp.int32) for index in range(slots)]
        found = tuple(known + each * block for known, each in zip(found, here))
        sizes = tuple(known + each * scalars[z, p, at, 1] for known, each in zip(sizes, here))
        return (count + own, found, sizes)

    nothing = (jnp.int32(0),) * slots
    _, found, sizes = lax.fori_loop(0, total_blocks, look, (jnp.int32(0), nothing, nothing))
    pump.work(3.0)
    pump.until(pieces[2])
    pump.until(pieces[3])
    keep("near")
    enc_sent.wait_recv()
    place_in = lax.broadcasted_iota(jnp.int32, (KB, 128), 0)
    for index in range(slots):
        here = pl.ds(index * KB, KB)
        z, p, at = block_at(found[index])
        for half in range(2):
            enc_mine[here, pl.ds(half * half_cols, half_cols)] = enc[half, z, p, at]
        mask[here, :] = jnp.where(place_in < sizes[index], 0.0, masked_score).astype(BF)
    keep("enc_mine", "mask")
    pump.work(1.0)
    q2[...] = dot(h2[...], columns_of(near, 2, 0, width)).astype(BF)
    kc[...] = dot(enc_mine[...], columns_of(near, 2, width, width)).astype(BF)
    vc[...] = dot(enc_mine[...], columns_of(near, 3, 0, width)).astype(BF)
    keep("q2", "kc", "vc")
    pump.work(4.0)
    for pair in range(width // 128):
        cross_forward(
            pair, q2, kc, vc, mask, o2, o2_turned, lse2, eye, scores, low_probs,
            lambda: pump.work(2.5),
        )
    keep("lse2", "o2", "o2_turned")
    two_sent = swap_rows(copies, place, part_two, got_two, o2, [columns_of(near, 3, width, width)])
    pump.work(1.0)
    @row_tiles(length)
    def _(tile):
        arrived(two_sent, tile)
        rows = rows_of(tile)
        values = x1[rows, :] + both_parts(part_two, got_two, rows)
        x2[rows, :] = values
        h3[rows, :] = norm_rows(values, gains[2:3, :]).astype(BF)

    h3_turned[...] = turn(h3[...], eye)
    pump.work(4.0)
    for tile in range(feed.shape[0]):
        pump.until(pieces[4 + tile])
        feed_tile(
            tile, h3, df, h3_turned, df_turned, feed, y_part, dn_part, g_feed,
            FEED_TILE, gate_up, dhidden, hidden, dpair,
        )
        moves.start(("g_feed", tile), g_feed.at[tile], outs["g_feed"].at[tile])
        pump.work(5.0)
    pump.drain()
    dn_sent = []
    for start in (0, 256):
        rows = pl.ds(start, 256)
        dn_low[rows, :] = dn_part[rows, :].astype(BF)
        dn_sent.append(copies.remote(dn_low.at[rows, :], got_dn.at[rows, :], place.sibling))
    other_rows = pl.ds(pl.multiple_of((1 - place.core) * half_rows, half_rows), half_rows)
    y_low[...] = y_part[...].astype(BF)
    y_sent = copies.remote(y_low.at[other_rows, :], got_y, place.sibling)
    stats[...] = jnp.zeros_like(stats)

    @row_tiles(length)
    def _(tile):
        arrived(dn_sent, tile)
        rows = rows_of(tile)
        delta, gain = back_through_norm(
            x2[rows, :], gains[2:3, :], both_parts(dn_low, got_dn, rows)
        )
        dx2[rows, :] = df[rows, :].astype(F32) + delta
        stats[0:1, :] += gain

    keep("dx2")
    y_sent.wait_recv()

    @row_tiles(half_rows)
    def _(tile):
        rows = rows_of(tile)
        start = pl.multiple_of(place.core * half_rows + tile * 64, 64)
        here = pl.ds(start, 64)
        values = x2[here, :] + (y_low[here, :].astype(F32) + got_y[rows, :].astype(F32))
        layer_out[rows, :] = values.astype(BF)
        row = lax.broadcasted_iota(jnp.int32, (64, 1), 0) + start
        stats[1:2, :] += jnp.sum(jnp.where(row < top, values * values, 0.0), axis=0, keepdims=True)

    keep("layer_out", "stats")
    moves.finish()
    copies.finish()


def front_shapes(blocks, slots, length, width, rows, pieces):
    long = blocks // 4
    heads = width // DH
    tiles = length // 128
    keys = slots * KB
    return {
        "near": ((pieces, long, 4, rows, PIECE), BF),
        "bias": ((heads * tiles, 128, 128), F32),
        "h1_turned": ((D, length), BF),
        "qkv": ((length, 3 * width), BF),
        "lse1": ((8, length), F32),
        "o1": ((length, width), BF),
        "o1_turned": ((width, length), F32),
        "x1": ((length, D), F32),
        "h2_turned": ((D, length), BF),
        "q2": ((length, width), BF),
        "enc_mine": ((keys, D), BF),
        "kc": ((keys, width), BF),
        "vc": ((keys, width), BF),
        "mask": ((keys, 128), BF),
        "lse2": ((8, length), F32),
        "o2": ((length, width), BF),
        "o2_turned": ((width, length), F32),
        "dx2": ((length, D), F32),
        "g_feed": ((pieces, long, 4, rows, PIECE), BF),
        "layer_out": ((length // 2, D), BF),
        "stats": ((8, D), F32),
    }


SMEM = pl.BlockSpec(memory_space=pltpu.SMEM)


def front(blocks, slots, shapes, operands, scalars, per_chip):
    levels = int(math.log2(blocks)) - 2
    long = blocks // 4
    length = shapes["x1"][0][0]
    pieces, rows = shapes["near"][0][0], shapes["near"][0][3]
    keys = slots * KB
    count = (2 * pieces + 2) * (levels + 3) + 12
    outs = tuple(jax.ShapeDtypeStruct(*shapes[name]) for name in FRONT_OUT)
    wide = pltpu.VMEM((length, D), F32)
    low = pltpu.VMEM((length, D), BF)
    return pl.pallas_call(
        functools.partial(front_kernel, levels, slots),
        out_shape=outs + (jax.ShapeDtypeStruct((blocks * per_chip,), jnp.int32),),
        in_specs=[VMEM] * len(operands) + [SMEM] * len(scalars),
        out_specs=(ANY,) * len(outs) + (SMEM,),
        scratch_shapes=[pltpu.VMEM(*shapes[name]) for name in FRONT_OUT]
        + [
            pltpu.VMEM((2, keys, 256), F32),
            pltpu.VMEM((2, keys, 256), BF),
            pltpu.VMEM((length, 2 * FEED_TILE), F32),
            pltpu.VMEM((length, FEED_TILE), F32),
            pltpu.VMEM((length, FEED_TILE), BF),
            pltpu.VMEM((length, 2 * FEED_TILE), BF),
            pltpu.VMEM(*shapes["near"]),
            pltpu.VMEM((2, long, 4, per_chip, KB, D // 2), BF),
            pltpu.VMEM((long, 4, 8, 128), jnp.int32),
            pltpu.SMEM((long, 4, 8, 128), jnp.int32),
            pltpu.VMEM((2, length // 2, D), BF),
            pltpu.VMEM((2, length // 2, D), BF),
            low, low, wide, wide, low, low, low, low,
            pltpu.VMEM((length // 2, D), BF),
            low, wide, low, low,
            pltpu.VMEM((D, length), BF),
            pltpu.VMEM((D, length), BF),
            pltpu.VMEM((256, 256), BF),
            pltpu.VMEM((16, 256 * (length // 128)), F32),
            low, low,
            pltpu.SemaphoreType.DMA((count,)),
            pltpu.SemaphoreType.DMA((count,)),
            pltpu.SemaphoreType.DMA((len(FRONT_OUT) + pieces + 1,)),
        ],
        compiler_params=pltpu.CompilerParams(
            collective_id=0, has_side_effects=True, vmem_limit_bytes=int(63.4 * 2**20)
        ),
    )(*operands, *scalars)


BACK_IN = (
    "g_feed", "near", "dx2", "o2", "q2", "kc", "vc", "mask", "lse2", "o2_turned", "h2_turned", "x1",
    "o1", "qkv", "bias", "lse1", "o1_turned", "h1_turned", "stats",
)


def put_product(ref, piece, start, turned, right, half):
    long = ref.shape[1] // 2
    value = dot(turned, right).astype(BF)
    value = value.reshape((long,) + ref.shape[2:4] + (value.shape[1],))
    ref[piece, pl.ds(long * half, long), :, :, pl.ds(start, value.shape[3])] = value


def put_outer(ref, targets, left, eye=None):
    for half in range(2):
        part = pl.ds(half * (D // 2), D // 2)
        turned = left[part, :] if eye is None else turn(left[:, part].astype(BF), eye)
        for piece, start, right in targets:
            put_product(ref, piece, start, turned, right[...], half)


def put_rows(ref, left, right, dims, add=False):
    for start in range(0, ref.shape[0], 256):
        rows = pl.ds(start, 256)
        value = dot(left[rows, :].astype(BF), right, dims)
        ref[rows, :] = (ref[rows, :] + value if add else value).astype(ref.dtype)


def back_kernel(
    levels, slots,
    gains, tok_own, buckets, slot_of, limit, enc_kept, *refs,
):
    sources = dict(zip(BACK_IN, refs))
    grad_out, decoder_grad, encoder_grad, sums, squares = refs[len(BACK_IN) : len(BACK_IN) + 5]
    refs = refs[len(BACK_IN) + 5 :]
    landed = dict(zip(BACK_IN, refs))
    (
        g_feed, near, dx2, o2, q2, kc, vc, mask, lse2, o2_turned, h2_turned, x1, o1, qkv, bias, lse1,
        o1_turned, h1_turned, stats,
    ) = refs[: len(BACK_IN)]
    (
        g_near, two, one, total, zs, line_two, line_one, line_total, line_zs, spread, e_two, e_one,
        e_total, e_zs, do, dq, dkc, dvc, dqkv, e_all, e_got, part, got_dn, got_half,
        bias_total, small, small_plane, small_middle, small_line, last, last_plane, last_middle,
        last_line, eye, scores, dprobs, low_probs, low_dscores, free, send, recv, local,
    ) = refs[len(BACK_IN) :]
    place = Place(levels)
    copies, moves = Copies(send, recv), Moves(local)
    near_pieces = near.shape[0]
    keys = slots * KB
    for name in BACK_IN:
        by_key = name in ("kc", "vc", "mask")
        source = sources[name].at[pl.ds(0, keys), :] if by_key else sources[name]
        moves.start(name, source, landed[name])
    enter(place.mates())
    pump = Pump("xy", 15.0, 50.0, 0.7)
    length, width = o1.shape
    half_rows = length // 2
    top = limit[0]
    half_cols = e_all.shape[3]

    def piece(index):
        source = View(g_near if index < near_pieces else g_feed, index % near_pieces)
        out = View(grad_out, index)
        if index == near_pieces:
            scratch = [View(ref) for ref in (line_two, line_one, line_total, line_zs)]
            return scatter_line_first(place, copies, source, *scratch, out)
        at = spot[index]
        scratch = [View(ref, at) for ref in (two, one, total, zs)]
        return scatter_chain(place, copies, source, *scratch, out)

    def half_piece(index, start):
        columns = pl.ds(start, width)
        scratch = [View(ref, spot[index], columns=columns) for ref in (two, one, total, zs)]
        return scatter_chain(
            place, copies, View(g_near, index, columns=columns), *scratch,
            View(grad_out, index, columns=columns),
        )

    spot = {5: 0, 6: 1, 7: 2, 2: 3, 3: 4, 0: 0, 1: 1}

    moves.need("g_feed")
    feed_chains = [piece(index) for index in range(near_pieces, near_pieces + g_feed.shape[0])]
    pump.add(*feed_chains)
    make_eye(eye)
    moves.need("near", "dx2", "o2")
    put_rows(do, dx2, columns_of(near, 3, width, width), NN)
    put_outer(g_near, [(3, width, o2)], dx2, eye)
    pump.work(2.5)
    moves.need("q2", "kc", "vc", "mask", "lse2", "o2_turned")
    for pair in range(width // 128):
        cross_backward(
            pair, q2, kc, vc, mask, lse2, o2_turned, do, dq, dkc, dvc, eye,
            scores, dprobs, low_probs, low_dscores, lambda: pump.work(4.0),
        )
    enc_mine = low_probs.at[:, pl.ds(0, D)]
    moves.start("enc_mine", enc_kept.at[pl.ds(0, keys), :], enc_mine)
    pump.work(2.0)
    dn_sent = swap_rows(copies, place, part, got_dn, dq, [columns_of(near, 2, 0, width)])
    half_long = near.shape[1] // 2
    for index in range(2):
        weights = [
            near[piece, half_long * index : half_long * (index + 1), :, :, pl.ds(start, width)]
            .reshape(half_cols, width)
            for piece, start in ((2, width), (3, 0))
        ]
        step = slots // 3 if slots % 3 == 0 else slots // 2
        for first in range(0, slots, step):
            here = pl.ds(first * KB, step * KB)
            term = dot(dkc[here, :], weights[0], NT) + dot(dvc[here, :], weights[1], NT)
            e_all[index, pl.ds(first, step)] = term.astype(BF).reshape(step, KB, half_cols)

    e_sent = copies.remote(
        e_all.at[1 - place.core, pl.ds(0, slots)], e_got, place.sibling
    )
    pump.work(2.0)
    moves.need("h2_turned")
    put_outer(g_near, [(2, 0, dq)], h2_turned)
    moves.need("enc_mine")
    put_outer(g_near, [(2, width, dkc), (3, 0, dvc)], low_probs, eye)
    pump.work(3.0)
    pump.add(piece(2), piece(3))
    e_sent.wait_recv()

    for index in range(slots):
        own = e_all[place.core, index].astype(F32)
        e_all[place.core, index] = (own + e_got[index].astype(F32)).astype(BF)

    e_all[place.core, slots] = jnp.zeros((KB, half_cols), BF)
    per_chip = spread.shape[2] // KB
    for block in range(spread.shape[0] * 4 * per_chip):
        chip, at = block // per_chip, block % per_chip
        spread[chip // 4, chip % 4, pl.ds(at * KB, KB), :] = e_all[place.core, slot_of[block]]
    scratch = [View(ref) for ref in (spread, e_two, e_one, e_total, e_zs, encoder_grad)]
    pump.add(scatter_chain(place, copies, *scratch))
    moves.need("x1")
    sums[...] = jnp.zeros_like(sums)
    bias_total[...] = jnp.zeros_like(bias_total)

    @row_tiles(length)
    def _(tile):
        arrived(dn_sent, tile)
        rows = rows_of(tile)
        delta, gain = back_through_norm(x1[rows, :], gains[1:2, :], both_parts(part, got_dn, rows))
        dx2[rows, :] = dx2[rows, :] + delta
        sums[1:2, :] += 0.5 * gain

    pump.work(4.0)
    moves.need(*BACK_IN)
    put_rows(do, dx2, columns_of(near, 1, width, width), NN)
    put_outer(g_near, [(1, width, o1)], dx2, eye)
    pump.work(2.5)
    pump.until(feed_chains[1])
    pump.until(feed_chains[2])
    writers = [place.first, place.second] + [place.partner(level) for level in range(levels)]
    for device in writers:
        pl.semaphore_signal(free, inc=1, device_id=device, device_id_type=MESH)
    pl.semaphore_wait(free, len(writers))
    pump.add(half_piece(1, width))
    for pair in range(width // 128):
        self_backward(
            pair, qkv, bias, lse1, o1_turned, do, dqkv, buckets, bias_total, eye,
            scores, dprobs, low_probs, low_dscores, lambda: pump.work(2.5),
        )
    pump.work(1.0)
    put_outer(g_near, [(0, 0, dqkv.at[:, pl.ds(0, 2 * width)])], h1_turned)
    pump.add(half_piece(0, 0), half_piece(0, width))
    pump.work(1.0)
    put_outer(g_near, [(1, 0, dqkv.at[:, pl.ds(2 * width, width)])], h1_turned)
    pump.add(half_piece(1, 0))
    for copy in dn_sent:
        copies.left(copy)
    weights = [columns_of(near, 0, 0, 2 * width), columns_of(near, 1, 0, width)]
    for start in range(0, length, 256):
        rows = pl.ds(start, 256)
        total = dot(dqkv[rows, pl.ds(0, 2 * width)], weights[0], NT)
        total = total + dot(dqkv[rows, pl.ds(2 * width, width)], weights[1], NT)
        part[rows, :] = total.astype(BF)
    own_rows = pl.multiple_of(place.core * half_rows, half_rows)
    other_rows = pl.ds(pl.multiple_of((1 - place.core) * half_rows, half_rows), half_rows)
    half_sent = copies.remote(part.at[other_rows, :], got_half, place.sibling)
    pump.work(3.0)
    half_sent.wait_recv()
    sums[2:3, :] = 0.5 * stats[0:1, :]
    sums[3:4, :] = stats[1:2, :]

    @row_tiles(half_rows)
    def _(tile):
        rows = rows_of(tile)
        start = pl.multiple_of(own_rows + tile * 64, 64)
        here = pl.ds(start, 64)
        values = tok_own[rows, :].astype(F32)
        total = part[here, :].astype(F32) + got_half[rows, :].astype(F32)
        delta, gain = back_through_norm(values, gains[0:1, :], total)
        result = dx2[here, :] + delta
        decoder_grad[rows, :] = result
        row = lax.broadcasted_iota(jnp.int32, (64, 1), 0) + start
        sums[0:1, :] += gain
        sums[4:5, :] += jnp.sum(jnp.where(row < top, result * result, 0.0), axis=0, keepdims=True)
        sums[5:6, :] += jnp.sum(jnp.where(row < top, 1.0, 0.0), axis=0, keepdims=True) * jnp.ones((1, D), F32)

    rows_bias = bias_total[...]
    for index in range(2):
        keep = jnp.where(place.core == index, 1.0, 0.0)
        sums[pl.ds(8 + 8 * index, 8), pl.ds(0, 128)] = rows_bias * keep
    small[...] = sums[...]
    pump.add(sum_chain(place, copies, small, small_plane, small_middle, small_line, sums))
    pump.drain()
    square = jnp.zeros((8, 128), F32)
    for index in range(grad_out.shape[0]):
        for start in range(0, PIECE, 128):
            tile = grad_out[index, :, pl.ds(start, 128)]
            tile = tile * tile
            for row in range(0, tile.shape[0], 8):
                square = square + tile[row : row + 8]
    last[...] = square
    pump.add(sum_chain(place, copies, last, last_plane, last_middle, last_line, squares))
    pump.drain()
    copies.finish()


def back(blocks, slots, shapes, made, tok_own, gains, limit, buckets, key_rows):
    levels = int(math.log2(blocks)) - 2
    long = blocks // 4
    pieces, rows = shapes["near"][0][0], shapes["near"][0][3]
    length, width = shapes["o1"][0]
    keys = slots * KB
    half = D // 2
    by_name = dict(zip(FRONT_OUT, made))

    def landing(name):
        dims, kind = shapes[name]
        return ((keys,) + dims[1:] if name in ("kc", "vc", "mask") else dims, kind)

    count = (2 * pieces + 3) * (levels + 3) + 4 + 2 * (7 + long - 1)
    shape = lambda *dims: jax.ShapeDtypeStruct(dims, F32)
    outs = (
        shape(2 * pieces, rows, PIECE),
        shape(length // 2, D),
        shape(key_rows, half),
        shape(24, D),
        shape(8, 128),
    )
    steps = 2**levels - 1
    usual = 5
    block = (rows, PIECE)
    enc_block = (key_rows, half)
    sizes = [shapes["near"]]
    sizes += [((usual,) + lead + block, BF) for lead in ((2, long), (long,), (long,), (steps,))]
    sizes += [(lead + block, BF) for lead in ((2,), (), (long // 2, 4), (steps, 4))]
    sizes += [
        (lead + enc_block, BF) for lead in ((long, 4), (2, long), (long,), (long,), (steps,))
    ]
    sizes += [
        ((length, width), BF), ((length, width), BF), ((keys, width), BF), ((keys, width), BF),
        ((length, 3 * width), BF), ((2, slots + 1, KB, half), BF),
        ((slots, KB, half), BF), ((length, D), BF), ((length, D), BF), ((length // 2, D), BF),
        ((8, 128), F32),
    ]
    for member in ((24, D), (8, 128)):
        sizes += [(lead + member, F32) for lead in ((), (8,), (), (long,))]
    sizes += [
        ((256, 256), BF), ((2, keys, 256), F32), ((2, keys, 256), F32), ((keys, 2 * length), BF),
        ((keys, 2 * length), BF),
    ]
    return pl.pallas_call(
        functools.partial(back_kernel, levels, slots),
        out_shape=outs,
        in_specs=[VMEM, VMEM, VMEM, SMEM, SMEM] + [ANY] * (len(BACK_IN) + 1),
        out_specs=(VMEM,) * 5,
        scratch_shapes=[pltpu.VMEM(*landing(name)) for name in BACK_IN]
        + [pltpu.VMEM(*size) for size in sizes]
        + [
            pltpu.SemaphoreType.REGULAR,
            pltpu.SemaphoreType.DMA((count,)),
            pltpu.SemaphoreType.DMA((count,)),
            pltpu.SemaphoreType.DMA((len(BACK_IN) + 1,)),
        ],
        compiler_params=pltpu.CompilerParams(
            collective_id=1, has_side_effects=True, vmem_limit_bytes=int(63.4 * 2**20)
        ),
    )(
        gains, tok_own, buckets, made[-1], limit, by_name["enc_mine"],
        *(by_name[name] for name in BACK_IN),
    )


def adam_kernel(grads, sums, squares, *refs):
    params, firsts, seconds, passed = refs[:8], refs[8:16], refs[16:24], refs[24:27]
    news, new_firsts, new_seconds = refs[27:35], refs[35:43], refs[43:51]
    norm_ref, rms_ref = refs[51:53]
    for index in range(3):
        refs[53 + index][...] = passed[index][...]
    width = params[0].shape[2]
    heads, known = params[7].shape
    gains = sums[0:3, :]
    by_head = jnp.concatenate(
        [sums[8 : 8 + heads // 2, 0:128], sums[16 : 16 + heads // 2, 0:128]], axis=0
    )[:, :known]
    whole = lambda value: jnp.sum(jnp.sum(value, axis=1, keepdims=True), axis=0, keepdims=True)
    norm = jnp.sqrt(whole(squares[...]) + whole(gains * gains) + whole(by_head * by_head))
    factor = jnp.minimum(1.0, clip_limit / (norm + 1e-06))
    norm_ref[...] = norm
    counted = sums[5:6, 0:1] * D
    rms_ref[...] = jnp.concatenate(
        [jnp.sqrt(whole(sums[3:4, :]) / counted), jnp.sqrt(whole(sums[4:5, :]) / counted)], axis=1
    )

    def update(index, at, grad):
        decay = weight_decay if index < 6 else 0.0
        weight, moment, second = adamw(
            params[index][at], firsts[index][at], seconds[index][at], grad * factor, decay,
            learn_rates[index],
        )
        news[index][at] = weight
        new_firsts[index][at] = moment
        new_seconds[index][at] = second

    columns = lambda piece, start, count: grads[piece, :, pl.ds(start, count)]
    for index, base in ((0, 0), (2, 2)):
        update(index, (0,), columns(base, 0, width))
        update(index, (1,), columns(base, width, width))
        update(index, (2,), columns(base + 1, 0, width))
        update(index + 1, (slice(None),), columns(base + 1, width, width))
    for tile in range(params[5].shape[1] // FEED_TILE):
        at = pl.ds(tile * FEED_TILE, FEED_TILE)
        for part in range(2):
            update(4, (part, slice(None), at), columns(4 + tile, part * FEED_TILE, FEED_TILE))
        update(5, (slice(None), at), columns(4 + tile, 2 * FEED_TILE, FEED_TILE))
    update(6, (slice(None),), gains)
    update(7, (slice(None),), by_head)


TURNED = (1, 3, 5, 7)


def turned_views(group):
    return [member.T if index in TURNED else member for index, member in enumerate(group)]


def adam(grads, sums, squares, params, firsts, seconds, passed):
    params, firsts, seconds = (turned_views(group) for group in (params, firsts, seconds))
    same = [jax.ShapeDtypeStruct(member.shape, F32) for member in params]
    outs = same * 3 + [jax.ShapeDtypeStruct((1, 1), F32), jax.ShapeDtypeStruct((1, 2), F32)]
    outs += [jax.ShapeDtypeStruct(member.shape, member.dtype) for member in passed]
    made = pl.pallas_call(
        adam_kernel,
        out_shape=tuple(outs),
        in_specs=[VMEM] * 30,
        out_specs=(VMEM,) * 29,
        compiler_params=pltpu.CompilerParams(vmem_limit_bytes=60 * 2**20),
    )(grads, sums, squares, *params, *firsts, *seconds, *passed)
    groups = [turned_views(made[start : start + 8]) for start in (0, 8, 16)]
    return (sum(groups, []), made[24], made[25], made[26:])


def fused(*args):
    (decoder_in, encoder_out, out_grad, block_items, block_lengths, target_lengths) = args[:6]
    params, firsts, seconds = args[6:14], args[14:22], args[22:30]
    norm_gains, position_bias = params[6:]
    blocks = lax.axis_size("blk")
    length = 2 * decoder_in.shape[0]
    key_rows = encoder_out.shape[0]
    width = params[0].shape[2]
    rows = params[0].shape[1]
    per_chip = key_rows // KB
    total_blocks = blocks * per_chip
    most = total_blocks - blocks * target_lengths.shape[0] + 1
    slots = -(-most // 6) * 6
    tiles = length // 128
    offsets = np.arange(256)
    steps = np.where(offsets < 128, offsets, offsets - 256)[None] + 128 * np.arange(tiles)[:, None]
    one_hot = np.eye(position_bias.shape[0], dtype=np.float32)[bucket_of(np.maximum(steps, 0))]
    one_hot = one_hot * (steps >= 0)[..., None]
    buckets = np.zeros((tiles, 256, 128), np.float32)
    buckets[:, :, : one_hot.shape[2]] = one_hot
    blank = np.where(steps >= 0, 0.0, masked_score).astype(np.float32).reshape(1, -1)
    shapes = front_shapes(blocks, slots, length, width, rows, 8 * width // PIECE)
    weights = turned_views(params)[:6]
    operands = weights + [
        encoder_out, decoder_in, out_grad, norm_gains, position_bias.T,
        jnp.asarray(one_hot.reshape(tiles * 256, -1).T), jnp.asarray(blank),
    ]
    scalars = [block_items, block_lengths, target_lengths]
    made = front(blocks, slots, shapes, operands, scalars, per_chip)
    grads, decoder_grad, encoder_grad, sums, squares = back(
        blocks, slots, shapes, made, decoder_in, norm_gains, target_lengths,
        jnp.asarray(buckets, BF), key_rows,
    )
    layer_out = made[FRONT_OUT.index("layer_out")]
    updated, norm, rms, passed = adam(
        grads, sums, squares, params, firsts, seconds, [layer_out, decoder_grad, encoder_grad]
    )
    return (*passed, *updated, norm.reshape(()), rms.reshape(2))


def plain_body(
    decoder_in,
    encoder_out,
    out_grad,
    block_items,
    block_lengths,
    target_lengths,
    self_proj,
    self_out,
    cross_proj,
    cross_out,
    feed_in,
    feed_out,
    norm_gains,
    position_bias,
    *moments,
):
    core = lax.axis_index("mp")
    rank = lax.axis_index("blk")
    blocks = lax.axis_size("blk")
    rows_own = decoder_in.shape[0]
    length = 2 * rows_own
    half = self_proj.shape[2]
    heads = half // DH
    hidden_half = feed_in.shape[2]
    key_rows = encoder_out.shape[0]

    params = [self_proj, self_out, cross_proj, cross_out, feed_in, feed_out]
    flat = []
    for value in params:
        if value.ndim == 3:
            flat.extend(value[index].astype(BF) for index in range(value.shape[0]))
        else:
            flat.append(value.astype(BF).T)
    shard = jnp.concatenate(flat, axis=1)
    edges = np.cumsum([0] + [member.shape[1] for member in flat]).tolist()
    places = jnp.arange(key_rows, dtype=jnp.int32)
    tags_own = jnp.where(
        places % KB < jnp.repeat(block_lengths, KB), jnp.repeat(block_items, KB), -1
    )
    encoder_half = lax.dynamic_slice_in_dim(encoder_out, core * (D // 2), D // 2, 1)
    weights = lax.all_gather(shard, "blk", axis=0, tiled=True)
    encoder = lax.all_gather(encoder_out, "blk", axis=0, tiled=True)
    tags = lax.all_gather(tags_own, "blk", axis=0, tiled=True)
    tokens = lax.all_gather(decoder_in, "mp")
    upstream = lax.all_gather(out_grad, "mp")
    tokens = tokens.reshape(length, D).astype(F32)
    limit = target_lengths[0]
    valid = (jnp.arange(length, dtype=jnp.int32) < limit).astype(F32)[:, None]
    dy = upstream.reshape(length, D).astype(F32) * valid
    w_q, w_k, w_v, w_so, c_q, c_k, c_v, w_co, f_g, f_u, f_d = (
        weights[:, edges[index] : edges[index + 1]] for index in range(11)
    )

    def both(term):
        pair = lax.all_gather(term, "mp")
        return pair[0] + pair[1]

    def dot(left, right, dims=((1,), (0,))):
        return lax.dot_general(left, right, (dims, ((), ())), preferred_element_type=F32)

    NT = ((1,), (1,))
    TN = ((0,), (0,))
    h1 = rms_norm(tokens, norm_gains[0]).astype(BF)
    q1, k1, v1 = (dot(h1, w).astype(BF).reshape(length, heads, DH) for w in (w_q, w_k, w_v))
    bias_here = lax.dynamic_slice_in_dim(position_bias, core * heads, heads, 1)
    spots = np.arange(length)
    buckets = bucket_of(np.maximum(spots, 0))
    by_distance = jnp.dot(
        jnp.asarray(np.eye(position_bias.shape[0], dtype=np.float32)[buckets]),
        bias_here,
        precision=HIGHEST,
    )
    tiles = length // 128
    offsets = np.arange(256)
    steps = np.where(offsets < 128, -offsets, 256 - offsets)[None] + 128 * np.arange(tiles)[:, None]
    strips = jnp.where(
        steps[None] >= 0, by_distance.T[:, np.maximum(np.minimum(steps, length - 1), 0)], masked_score
    )
    diagonals = pl.pallas_call(
        toeplitz_kernel,
        out_shape=jax.ShapeDtypeStruct((heads * tiles, 128, 128), F32),
        in_specs=[VMEM],
        out_specs=VMEM,
    )(strips.reshape(heads * tiles, 1, 256)).reshape(heads, tiles, 128, 128)
    blank = jnp.full((heads, 128, 128), masked_score)
    bias = jnp.concatenate(
        [
            jnp.concatenate([diagonals[:, i - j] if i >= j else blank for j in range(tiles)], 2)
            for i in range(tiles)
        ],
        1,
    )
    s1 = jnp.einsum("qhd,khd->hqk", q1, k1, preferred_element_type=F32) + bias
    p1 = jnp.exp(s1 - jnp.max(s1, -1, keepdims=True))
    p1 = p1 / jnp.sum(p1, -1, keepdims=True)
    p1_low = p1.astype(BF)
    o1 = jnp.einsum("hqk,khd->qhd", p1_low, v1, preferred_element_type=F32).astype(BF)
    o1 = o1.reshape(length, half)
    x1 = tokens + both(dot(o1, w_so, NT))
    h2 = rms_norm(x1, norm_gains[1]).astype(BF)
    q2 = dot(h2, c_q).astype(BF).reshape(length, heads, DH)
    total_blocks = tags.shape[0] // KB
    items = blocks * target_lengths.shape[0]
    most = total_blocks - items + 1
    owned = tags.reshape(total_blocks, KB)[:, 0] == rank
    order = jnp.argsort(jnp.logical_not(owned), stable=True)[:most]
    enc = encoder.reshape(total_blocks, KB, D)[order].reshape(most * KB, D)
    mine = (tags.reshape(total_blocks, KB)[order].reshape(most * KB) == rank)
    kc = dot(enc, c_k).astype(BF).reshape(-1, heads, DH)
    vc = dot(enc, c_v).astype(BF).reshape(-1, heads, DH)

    def cross_forward(parts):
        q, k, v = parts
        s = jnp.where(mine[None], dot(q, k, NT), masked_score)
        top = jnp.max(s, -1, keepdims=True)
        e = jnp.exp(s - top)
        total = jnp.sum(e, -1, keepdims=True)
        return (dot((e / total).astype(BF), v).astype(BF), top + jnp.log(total))

    by_head = lambda value: jnp.swapaxes(value.reshape(value.shape[0], heads, DH), 0, 1)
    q2h, kch, vch = by_head(q2), by_head(kc), by_head(vc)
    o2, lse = lax.map(cross_forward, (q2h, kch, vch))
    o2 = jnp.swapaxes(o2, 0, 1).reshape(length, half)
    x2 = x1 + both(dot(o2, w_co, NT))
    h3 = rms_norm(x2, norm_gains[2]).astype(BF)
    gate, upper = dot(h3, f_g), dot(h3, f_u)
    hidden_full, pull = jax.vjp(lambda g, u: jax.nn.gelu(g, approximate=True) * u, gate, upper)
    hidden = hidden_full.astype(BF)
    y = x2 + both(dot(hidden, f_d, NT))
    df = dy.astype(BF)
    g_fd = dot(df, hidden, TN)
    dgate, dup = (member.astype(BF) for member in pull(dot(df, f_d)))
    g_fg, g_fu = dot(h3, dgate, TN), dot(h3, dup, TN)
    dn3 = both(dot(dgate, f_g, NT) + dot(dup, f_u, NT))
    delta, gain3 = norm_back(x2, norm_gains[2], dn3)
    dx2 = dy + delta
    da2 = dx2.astype(BF)
    g_co = dot(da2, o2, TN)
    do2 = dot(da2, w_co).astype(BF)

    def cross_backward(parts):
        q, k, v, do, total = parts
        s = jnp.where(mine[None], dot(q, k, NT), masked_score)
        p = jnp.exp(s - total)
        dp = dot(do, v, NT)
        ds = (p * (dp - jnp.sum(p * dp, -1, keepdims=True))).astype(BF)
        return (
            dot(ds, k).astype(BF), dot(ds, q, TN).astype(BF), dot(p.astype(BF), do, TN).astype(BF)
        )

    dq2, dkc, dvc = lax.map(cross_backward, (q2h, kch, vch, by_head(do2), lse))
    flat_heads = lambda value: jnp.swapaxes(value, 0, 1).reshape(-1, half)
    dq2, dkc, dvc = flat_heads(dq2), flat_heads(dkc), flat_heads(dvc)
    g_cq, g_ck, g_cv = dot(h2, dq2, TN), dot(enc, dkc, TN), dot(enc, dvc, TN)
    enc_term = dot(dkc, c_k, NT) + dot(dvc, c_v, NT)
    spread = jnp.zeros((total_blocks, KB, D), BF).at[order].set(
        enc_term.astype(BF).reshape(most, KB, D)
    )
    encoder_grad = lax.psum_scatter(
        lax.psum_scatter(spread.reshape(-1, D), "mp", scatter_dimension=1, tiled=True),
        "blk", scatter_dimension=0, tiled=True,
    ).astype(F32)
    dn2 = both(dot(dq2, c_q, NT))
    delta, gain2 = norm_back(x1, norm_gains[1], dn2)
    dx1 = dx2 + delta
    da1 = dx1.astype(BF)
    g_so = dot(da1, o1, TN)
    do1 = dot(da1, w_so).astype(BF).reshape(length, heads, DH)
    dp1 = jnp.einsum("qhd,khd->hqk", do1, v1, preferred_element_type=F32)
    ds1 = (p1 * (dp1 - jnp.sum(p1 * dp1, -1, keepdims=True))).astype(BF)
    ds_wide = ds1.astype(F32)
    bucket_grid = jnp.asarray(bucket_of(np.maximum(spots[:, None] - spots[None, :], 0)).astype(np.int32))
    bias_sums = lax.map(
        lambda b: jnp.sum(jnp.where(bucket_grid[None] == b, ds_wide, 0.0), axis=(1, 2)),
        jnp.arange(position_bias.shape[0], dtype=jnp.int32),
    )
    grad_bias = lax.dynamic_update_slice_in_dim(
        jnp.zeros(position_bias.shape, F32), bias_sums, core * heads, 1
    )
    dq1 = jnp.einsum("hqk,khd->qhd", ds1, k1, preferred_element_type=F32)
    dk1 = jnp.einsum("hqk,qhd->khd", ds1, q1, preferred_element_type=F32)
    dv1 = jnp.einsum("hqk,qhd->khd", p1_low, do1, preferred_element_type=F32)
    dq1, dk1, dv1 = (member.astype(BF).reshape(length, half) for member in (dq1, dk1, dv1))
    g_q, g_k, g_v = dot(h1, dq1, TN), dot(h1, dk1, TN), dot(h1, dv1, TN)
    dn1 = both(dot(dq1, w_q, NT) + dot(dk1, w_k, NT) + dot(dv1, w_v, NT))
    delta, gain1 = norm_back(tokens, norm_gains[0], dn1)
    decoder_grad = dx1 + delta
    grads = jnp.concatenate(
        [member.astype(BF) for member in (g_q, g_k, g_v, g_so, g_cq, g_ck, g_cv, g_co, g_fg, g_fu, g_fd)],
        axis=1,
    )
    mine_grad = lax.psum_scatter(grads.astype(F32), "blk", scatter_dimension=0, tiled=True)
    pieces = [mine_grad[:, edges[index] : edges[index + 1]] for index in range(11)]
    shards = (
        jnp.stack(pieces[0:3]), pieces[3].T, jnp.stack(pieces[4:7]), pieces[7].T,
        jnp.stack(pieces[8:10]), pieces[10].T,
    )
    square_sum = jnp.sum(mine_grad * mine_grad)
    stat_terms = jnp.stack(
        [jnp.sum(valid * y * y), jnp.sum(valid * decoder_grad * decoder_grad), jnp.sum(valid)]
    )
    gain_grads, bias_grads, square_total, stat_total = lax.psum(
        (jnp.stack([gain1, gain2, gain3]) * 0.5, grad_bias, square_sum, stat_terms), ("blk", "mp")
    )
    grad_norm = jnp.sqrt(
        square_total + jnp.sum(gain_grads * gain_grads) + jnp.sum(bias_grads * bias_grads)
    )
    factor = jnp.minimum(1.0, clip_limit / (grad_norm + 1e-06))
    params = params + [norm_gains, position_bias]
    gradients = shards + (gain_grads, bias_grads)
    updated = [
        adamw(
            params[index], moments[index], moments[8 + index], gradients[index] * factor,
            weight_decay if index < 6 else 0.0, learn_rates[index],
        )
        for index in range(8)
    ]
    token_rms = jnp.sqrt(stat_total[:2] / (stat_total[2] * D))
    own = lambda value: lax.dynamic_slice_in_dim(value, core * rows_own, rows_own, 0)
    return (
        own(y).astype(BF),
        own(decoder_grad),
        encoder_grad,
        *(entry[0] for entry in updated),
        *(entry[1] for entry in updated),
        *(entry[2] for entry in updated),
        grad_norm,
        token_rms,
    )


def solution(mesh):
    proj, out = P(None, "blk", "mp"), P("mp", "blk")
    family = (proj, out, proj, out, proj, out, P(), P())
    tokens = P(("blk", "mp"), None)
    tiled = mesh.shape["blk"] == 16 and D // mesh.shape["blk"] % 16 == 0
    return jax.shard_map(
        fused if tiled else plain_body,
        mesh=mesh,
        in_specs=(tokens, P("blk", None), tokens, P("blk"), P("blk"), P("blk")) + family * 3,
        out_specs=(tokens, tokens, P("blk", "mp")) + family * 3 + (P(), P()),
        check_vma=False,
    )
```
